32 devices in a mesh: groups: 2 (over x), row: 16 (over z, y, core).
Axes of the slice: x: 2, y: 2, z: 4, core: 2. Of those that a mesh axis runs over, the one named last changes fastest.
Arguments:
- features: bfloat16 [128, 64, 512], P(('groups', 'row')), parts along dimension 0, may hold values from -6 to 6
- cotangent: bfloat16 [128, 64, 512], P(('groups', 'row')), parts along dimension 0, may hold values from -6 to 6
- depth_weight: bfloat16 [49, 512], P(None, 'row'), may hold values from -0.875 to 0.875
- depth_bias: bfloat16 [512], P('row'), may hold values from -3 to 3
- norm_gain: bfloat16 [512], P('row'), may hold values from 0.25 to 1.75
- norm_shift: bfloat16 [512], P('row'), may hold values from -3 to 3
- up_weight: bfloat16 [512, 2048], P('row'), may hold values from -0.25 to 0.25
- up_bias: bfloat16 [2048], P('row'), may hold values from -3 to 3
- down_weight: bfloat16 [2048, 512], P('row'), may hold values from -0.125 to 0.125
- down_bias: bfloat16 [512], P('row'), may hold values from -3 to 3
Outputs:
- block_out: bfloat16 [128, 64, 512], P(('groups', 'row')), parts along dimension 0
- grad_features: bfloat16 [128, 64, 512], P(('groups', 'row')), parts along dimension 0
- grad_up_weight: float32 [1024, 2048], P(('groups', 'row')), parts along dimension 0
- grad_down_weight: float32 [4096, 512], P(('groups', 'row')), parts along dimension 0
- grad_depth_weight: float32 [98, 512], P('groups', 'row'), parts along dimension 0
- grad_depth_bias: float32 [1024], P(('groups', 'row')), parts along dimension 0
- grad_norm_gain: float32 [1024], P(('groups', 'row')), parts along dimension 0
- grad_norm_shift: float32 [1024], P(('groups', 'row')), parts along dimension 0
- grad_up_bias: float32 [4096], P(('groups', 'row')), parts along dimension 0
- grad_down_bias: float32 [1024], P(('groups', 'row')), parts along dimension 0
The draws below stay inside these ranges and needn't reach their ends.
There are 2 independent parts, one for each index of `groups`. The reference program is written for one: setup_inputs(seed, part) draws one part's arguments, and reference() takes and returns one part's arrays. A program takes and returns all parts, laid end to end along the dimension named above; an argument that names none is the same for every part. Nothing has to cross between parts.
All inputs are finite; a program needn't handle non-finite values.
Results may differ from the reference program's by a relative error of at most 0.0055.
Values may be sent and summed in bfloat16 or wider, within the bound.
No kernel may reach another device: no remote copies, remote signals or barrier semaphores. Data moves between devices by JAX's collectives and lax.ppermute only.
A program may use at most 64 MiB of HBM per device.

```python
import math
import jax
import jax.numpy as jnp
from jax import lax

C = 512
HID = 2048
COLS = 64
H = 64
TOKENS = 4096


def with_spikes(result, key, source, target, shards_of, factor):
    def block_of(axis_at):
        return (jnp.arange(result.shape[axis_at]) // (result.shape[axis_at] // shards_of)).reshape((-1,) + (1,) * (result.ndim - 1 - axis_at))

    one_side = jax.random.permutation(key, shards_of)[block_of(target)]
    far = (block_of(target) + shards_of // 2) % shards_of
    return jnp.where((block_of(source) == one_side) | (block_of(source) == far), factor * result, result)


def steps_of(own_key, dims, pieces, low, largest):
    level, own = 1.0, jax.random.fold_in(own_key, 6)
    for position, parts in pieces:
        draws = jnp.exp(jax.random.uniform(jax.random.fold_in(own, position), (parts,), jnp.float32, low / len(pieces), largest / len(pieces)))
        level = level * jnp.repeat(draws, dims[position] // parts).reshape([-1 if axis == position else 1 for axis in range(len(dims))])
    return level


def scatter_about(own_key, shape, spread, reach, split=(), kind=jnp.bfloat16):
    entries = jax.random.normal(own_key, shape, jnp.float32) * spread
    if len(split) > 0:
        entries = steps_of(own_key, shape, split, -0.22, 0.18) * entries
    return jnp.clip(entries, min=-reach, max=reach).astype(kind)


def noise_with(stream_key, dims, scale, reach, pieces, heavy, kind=jnp.bfloat16):
    drawn = scale * jax.random.normal(stream_key, dims, jnp.float32)
    if pieces:
        drawn = drawn * steps_of(stream_key, dims, pieces, -0.22, 0.18)
    return jnp.clip(with_spikes(drawn, jax.random.fold_in(stream_key, 3), *heavy), -reach, reach).astype(kind)


def setup_inputs(seed: int = 0, part: int = 0) -> dict:
    key_of = jax.random.split(jax.random.key(seed), 11)
    part_keys = jax.random.split(jax.random.fold_in(key_of[10], part), 11)
    features = noise_with(part_keys[0], (H, COLS, C), 1.0, 6.0, ((0, 16),), (0, 2, 16, 2.0))
    cotangent = noise_with(part_keys[1], (H, COLS, C), 1.0, 6.0, ((0, 16),), (0, 2, 16, 2.0))
    depth_weight = scatter_about(key_of[2], (49, C), 49 ** -0.5, 0.875, ((1, 16),))
    depth_bias = scatter_about(key_of[3], (C,), 0.5, 3.0, ((0, 16),))
    norm_gain = jnp.clip(1.0 + 0.15 * jax.random.normal(key_of[4], (C,), jnp.float32), 0.25, 1.75).astype(jnp.bfloat16)
    norm_shift = scatter_about(key_of[5], (C,), 0.5, 3.0, ((0, 16),))
    up_weight = scatter_about(key_of[6], (C, HID), C ** -0.5, 0.25, ((0, 16),))
    up_bias = scatter_about(key_of[7], (HID,), 0.5, 3.0, ((0, 16),))
    down_weight = scatter_about(key_of[8], (HID, C), HID ** -0.5, 0.125, ((0, 16),))
    down_bias = scatter_about(key_of[9], (C,), 0.5, 3.0, ((0, 16),))
    return dict(features=features, cotangent=cotangent, depth_weight=depth_weight, depth_bias=depth_bias, norm_gain=norm_gain, norm_shift=norm_shift, up_weight=up_weight, up_bias=up_bias, down_weight=down_weight, down_bias=down_bias)


eps = 1e-06

def gelu_value(value):
    return 0.5 * value * (1.0 + lax.erf(value * (1.0 / math.sqrt(2.0))))

def gelu_slope(value):
    cumulative = 0.5 * (1.0 + lax.erf(value * (1.0 / math.sqrt(2.0))))
    density = jnp.exp(-0.5 * value * value) * (1.0 / math.sqrt(2.0 * math.pi))
    return cumulative + value * density

def depth_conv(padded, kernel, height, width):
    total = jnp.zeros((height, width, kernel.shape[1]), jnp.float32)
    for first in range(7):
        for second in range(7):
            total = total + padded[first:first + height, second:second + width, :] * kernel[first * 7 + second]
    return total

def depth_conv_back(padded, kernel, height, width):
    total = jnp.zeros((height, width, kernel.shape[1]), jnp.float32)
    for first in range(7):
        for second in range(7):
            total = total + padded[6 - first:6 - first + height, 6 - second:6 - second + width, :] * kernel[first * 7 + second]
    return total

def reference(features, cotangent, depth_weight, depth_bias, norm_gain, norm_shift, up_weight, up_bias, down_weight, down_bias):
    height, width, chans = features.shape
    scale = 1.0 / math.sqrt(TOKENS)
    kernel = depth_weight.astype(jnp.float32)
    padded = jnp.pad(features.astype(jnp.float32), ((3, 3), (3, 3), (0, 0)))
    conv = depth_conv(padded, kernel, height, width) + depth_bias.astype(jnp.float32)
    mean_val = lax.optimization_barrier(jnp.mean(conv, axis=2, keepdims=True))
    centered = conv - mean_val
    var_val = lax.optimization_barrier(jnp.mean(centered * centered, axis=2, keepdims=True))
    inv = lax.rsqrt(var_val + eps)
    normed = centered * inv
    normal_out = (normed * norm_gain.astype(jnp.float32) + norm_shift.astype(jnp.float32)).astype(jnp.bfloat16)
    flat_norm = normal_out.reshape(height * width, chans)
    hidden = jnp.dot(flat_norm, up_weight, preferred_element_type=jnp.float32) + up_bias.astype(jnp.float32)
    act = gelu_value(hidden).astype(jnp.bfloat16)
    mixed = jnp.dot(act, down_weight, preferred_element_type=jnp.float32)
    block_out = (features.astype(jnp.float32) + (mixed + down_bias.astype(jnp.float32)).reshape(height, width, chans)).astype(jnp.bfloat16)
    flat_cot = cotangent.reshape(height * width, chans)
    grad_down_weight = jnp.dot(act.T, flat_cot, preferred_element_type=jnp.float32) * scale
    grad_down_bias = lax.optimization_barrier(jnp.sum(flat_cot.astype(jnp.float32), axis=0)) * scale
    dact = jnp.dot(flat_cot, down_weight.T, preferred_element_type=jnp.float32)
    dhidden = (dact * gelu_slope(hidden)).astype(jnp.bfloat16)
    grad_up_weight = jnp.dot(flat_norm.T, dhidden, preferred_element_type=jnp.float32) * scale
    grad_up_bias = lax.optimization_barrier(jnp.sum(dhidden.astype(jnp.float32), axis=0)) * scale
    dnorm = jnp.dot(dhidden, up_weight.T, preferred_element_type=jnp.float32).reshape(height, width, chans)
    grad_norm_gain = lax.optimization_barrier(jnp.sum(dnorm * normed, axis=(0, 1))) * scale
    grad_norm_shift = lax.optimization_barrier(jnp.sum(dnorm, axis=(0, 1))) * scale
    scaled = dnorm * norm_gain.astype(jnp.float32)
    dconv = inv * (scaled - lax.optimization_barrier(jnp.mean(scaled, axis=2, keepdims=True)) - normed * lax.optimization_barrier(jnp.mean(scaled * normed, axis=2, keepdims=True)))
    dconv = dconv.astype(jnp.bfloat16)
    dconv_wide = dconv.astype(jnp.float32)
    back_pad = jnp.pad(dconv_wide, ((3, 3), (3, 3), (0, 0)))
    grad_features = (cotangent.astype(jnp.float32) + depth_conv_back(back_pad, kernel, height, width)).astype(jnp.bfloat16)
    taps = []
    for first in range(7):
        for second in range(7):
            taps.append(lax.optimization_barrier(jnp.sum(dconv_wide * padded[first:first + height, second:second + width, :], axis=(0, 1))))
    grad_depth_weight = jnp.stack(taps, axis=0) * scale
    grad_depth_bias = lax.optimization_barrier(jnp.sum(dconv_wide, axis=(0, 1))) * scale
    return (block_out, grad_features, grad_up_weight, grad_down_weight, grad_depth_weight, grad_depth_bias, grad_norm_gain, grad_norm_shift, grad_up_bias, grad_down_bias)
```

```python
import functools
import math

import jax
import jax.numpy as jnp
from jax import lax
from jax.experimental import pallas as pl
from jax.experimental.pallas import tpu as pltpu
from jax.sharding import PartitionSpec as P

eps = 1e-06
lanes = 128
taps = 49
f32 = jnp.float32
bf16 = jnp.bfloat16
row_bias, row_gain, row_shift, row_down, row_up = 49, 50, 51, 52, 53


def round_up(value, unit):
    return (value + unit - 1) // unit * unit


def call(kernel, outs, args, scratch=(), mib=24, flops=1_000_000, moved=1_000_000):
    return pl.pallas_call(
        kernel,
        out_shape=[jax.ShapeDtypeStruct(shape, dtype) for shape, dtype in outs],
        in_specs=[pl.BlockSpec(memory_space=pltpu.VMEM)] * len(args),
        out_specs=[pl.BlockSpec(memory_space=pltpu.VMEM)] * len(outs),
        scratch_shapes=list(scratch),
        compiler_params=pltpu.CompilerParams(vmem_limit_bytes=mib * 1024 * 1024),
        cost_estimate=pl.CostEstimate(flops=flops, bytes_accessed=moved, transcendentals=0),
    )(*args)


def place(quads):
    index = lax.axis_index("row")
    return index // quads, lax.rem(index, quads)


def one_hot(rows, columns, offset):
    down = lax.broadcasted_iota(jnp.int32, (rows, columns), 0)
    across = lax.broadcasted_iota(jnp.int32, (rows, columns), 1)
    return (across == down + offset).astype(f32)


def pack_kernel(quads, layers, rows, dw, db, gain, shift, down, upb, up, *rest):
    packs, held = rest[:-1], rest[-1]
    layer, member = place(quads)
    own = dw.shape[1]
    width = packs[0].shape[1]
    part = upb.shape[1]
    held[...] = jnp.zeros_like(held)
    held[0:taps, :] = dw[...].astype(f32)
    held[row_bias : row_bias + 1, :] = db[...].astype(f32)
    held[row_gain : row_gain + 1, :] = gain[...].astype(f32)
    held[row_shift : row_shift + 1, :] = shift[...].astype(f32)
    held[row_down : row_down + 1, :] = down[...].astype(f32)
    spread = one_hot(own, width, lax.axis_index("row") * own).astype(bf16)
    small = jnp.dot(held[...].astype(bf16), spread, preferred_element_type=f32)
    along = one_hot(part, width, layer * part).astype(bf16)
    bias = jnp.dot(
        jnp.broadcast_to(upb[...], (8, part)).astype(bf16), along, preferred_element_type=f32
    )
    at = lax.broadcasted_iota(jnp.int32, (rows, width), 0)
    small = small + jnp.where(at == row_up + member, bias[0:1, :], 0.0)
    small = small.astype(bf16)
    wide = [up[:, i * part : (i + 1) * part] for i in range(layers * quads)]
    for other, pack in enumerate(packs):
        partner = jnp.bitwise_xor(member, other)
        pack[0:rows, :] = small
        if pack.shape[0] != rows + own or width != layers * part:
            pack[rows:, :] = jnp.zeros((pack.shape[0] - rows, width), bf16)
        for z in range(layers):
            piece = wide[z * quads]
            for s in range(1, quads):
                piece = jnp.where(partner == s, wide[z * quads + s], piece)
            pack[rows : rows + own, z * part : (z + 1) * part] = piece


def unpack_kernel(quads, rows, own, *refs):
    packs, (small, up) = refs[:-2], refs[-2:]
    _, member = place(quads)
    total = packs[0][0:rows, :].astype(f32)
    for pack in packs[1:]:
        total = total + pack[0:rows, :].astype(f32)
    small[...] = total.astype(bf16)
    for other, pack in enumerate(packs):
        block = pack[rows:, :].astype(f32)[0:own, 0 : up.shape[2]]
        up[jnp.bitwise_xor(member, other)] = block.astype(bf16)


def fill(padded, blocks, width):
    height = blocks[1].shape[0]
    rows, columns, chans = padded.shape
    zero = jnp.zeros((rows, 8, chans), f32)
    padded[:, 0:8, :] = zero
    padded[:, 8 + width :, :] = jnp.zeros((rows, columns - 8 - width, chans), f32)
    padded[0:3, 8 : 8 + width, :] = blocks[0][height - 3 :, :, :].astype(f32)
    padded[3 : 3 + height, 8 : 8 + width, :] = blocks[1][...].astype(f32)
    padded[3 + height :, 8 : 8 + width, :] = blocks[2][0:3, :, :].astype(f32)


def slide(padded, weights, height, width, at, flip):
    sums = [jnp.zeros((width, lanes), f32) for _ in range(height)]
    for second in range(7):
        for row in range(height + 6):
            piece = padded[row, 5 + second : 5 + second + width, at]
            for out in range(height):
                first = row - out
                if 0 <= first < 7:
                    tap = first * 7 + second
                    tap = taps - 1 - tap if flip else tap
                    sums[out] = sums[out] + piece * weights[tap : tap + 1, at]
    return sums


def conv_kernel(features, low, high, *refs):
    smalls, (normal, normed, inv, params, padded, conv) = refs[:-6], refs[-6:]
    height, width, chans = features.shape
    total = smalls[0][...].astype(f32)
    for small in smalls[1:]:
        total = total + small[...].astype(f32)
    params[...] = total
    fill(padded, (low, features, high), width)

    def chunk(i, carry):
        at = pl.ds(pl.multiple_of(i * lanes, lanes), lanes)
        sums = slide(padded, params, height, width, at, False)
        for out in range(height):
            conv[out * width : (out + 1) * width, at] = (
                sums[out] + params[row_bias : row_bias + 1, at]
            )
        return carry

    lax.fori_loop(0, chans // lanes, chunk, 0)

    def norm(i, carry):
        at = pl.ds(pl.multiple_of(i * width, width), width)
        value = conv[at, :]
        centered = value - jnp.mean(value, axis=1, keepdims=True)
        var = jnp.mean(centered * centered, axis=1, keepdims=True)
        scale = lax.rsqrt(var + eps)
        value = centered * scale
        normed[at, :] = value
        inv[at, :] = jnp.broadcast_to(scale, (width, lanes))
        normal[at, :] = (
            value * params[row_gain : row_gain + 1, 0:chans]
            + params[row_shift : row_shift + 1, 0:chans]
        ).astype(bf16)
        return carry

    lax.fori_loop(0, height, norm, 0)


def back_kernel(dconv, low, high, cotangent, params, out, padded):
    height, width, chans = dconv.shape
    fill(padded, (low, dconv, high), width)

    def chunk(i, carry):
        at = pl.ds(pl.multiple_of(i * lanes, lanes), lanes)
        sums = slide(padded, params, height, width, at, True)
        for row in range(height):
            out[row, :, at] = (cotangent[row, :, at].astype(f32) + sums[row]).astype(bf16)
        return carry

    lax.fori_loop(0, chans // lanes, chunk, 0)


def taps_kernel(
    quads, layers, scale, dconv, features, low, high, cotangent, norms, upb, *refs
):
    outs, (padded, grads) = refs[:-2], refs[-2:]
    height, width, chans = dconv.shape
    layer, member = place(quads)
    fill(padded, (low, features, high), width)
    grads[...] = jnp.zeros_like(grads)

    def fold(value):
        return jnp.sum(value.reshape(width // 8, 8, lanes), axis=0)

    def chunk(i, carry):
        at = pl.ds(pl.multiple_of(i * lanes, lanes), lanes)
        own = [dconv[row, :, at].astype(f32) for row in range(height)]
        for second in range(7):
            sums = [jnp.zeros((8, lanes), f32) for _ in range(7)]
            for row in range(height + 6):
                piece = padded[row, 5 + second : 5 + second + width, at]
                for out in range(height):
                    first = row - out
                    if 0 <= first < 7:
                        sums[first] = sums[first] + fold(own[out] * piece)
            for first in range(7):
                tap = first * 7 + second
                grads[tap : tap + 1, at] = (
                    jnp.sum(sums[first], axis=0, keepdims=True) * scale
                )
        total = fold(own[0])
        for row in range(1, height):
            total = total + fold(own[row])
        grads[row_bias : row_bias + 1, at] = jnp.sum(total, axis=0, keepdims=True) * scale
        total = fold(cotangent[0, :, at].astype(f32))
        for row in range(1, height):
            total = total + fold(cotangent[row, :, at].astype(f32))
        grads[row_down : row_down + 1, at] = jnp.sum(total, axis=0, keepdims=True) * scale
        grads[row_gain : row_gain + 1, at] = norms[0:1, at] * scale
        grads[row_shift : row_shift + 1, at] = norms[1:2, at] * scale
        return carry

    lax.fori_loop(0, chans // lanes, chunk, 0)
    part = upb.shape[1] // layers
    for z in range(layers):
        bias = upb[0:1, z * part : (z + 1) * part] * scale
        for s in range(quads):
            grads[row_up + s : row_up + s + 1, z * lanes : z * lanes + part] = jnp.where(
                member == s, bias, 0.0
            )
    for step, out in enumerate(outs):
        to = lax.rem(layer + step, layers)
        out[...] = grads[:, pl.ds(pl.multiple_of(to * lanes, lanes), lanes)]


def mlp_kernel(quads, layers, scale, params, *refs):
    normals, refs = refs[:quads], refs[quads:]
    cots, refs = refs[:quads], refs[quads:]
    ups, refs = refs[:layers], refs[layers:]
    downs, refs = refs[:layers], refs[layers:]
    grad_ups, refs = refs[:layers], refs[layers:]
    dnorms, refs = refs[:quads], refs[quads:]
    act, upb, down, up, total = refs
    layer, member = place(quads)
    cells, chans = normals[0].shape
    hidden_units = act.shape[1]
    part = hidden_units // layers
    for step in range(layers):
        source = lax.rem(layer - step + layers, layers)
        up[pl.ds(pl.multiple_of(source * lanes, lanes), lanes), :] = ups[step][...]
        down[pl.ds(pl.multiple_of(source * part, part), part), :] = downs[step][...]
    bias = params[row_up : row_up + 1, 0:hidden_units]
    for s in range(1, quads):
        bias = jnp.where(member == s, params[row_up + s : row_up + s + 1, 0:hidden_units], bias)
    bias_sum = jnp.zeros((1, hidden_units), f32)
    for i in range(quads):
        hidden = jnp.dot(normals[i][...], up[...], preferred_element_type=f32) + bias
        dact = lax.dot_general(
            cots[i][...], down[...], (((1,), (1,)), ((), ())), preferred_element_type=f32
        )
        cumulative = 0.5 * (1.0 + lax.erf(hidden * (1.0 / math.sqrt(2.0))))
        density = jnp.exp(-0.5 * hidden * hidden) * (1.0 / math.sqrt(2.0 * math.pi))
        act[i * cells : (i + 1) * cells, :] = (hidden * cumulative).astype(bf16)
        dhidden = (dact * (cumulative + hidden * density)).astype(bf16)
        bias_sum = bias_sum + jnp.sum(dhidden.astype(f32), axis=0, keepdims=True)
        dnorm = lax.dot_general(
            dhidden, up[...], (((1,), (1,)), ((), ())), preferred_element_type=f32
        )
        dnorms[i][...] = dnorm.astype(dnorms[i].dtype)
        grad = lax.dot_general(
            normals[i][...], dhidden, (((0,), (0,)), ((), ())), preferred_element_type=f32
        )
        total[...] = grad if i == 0 else total[...] + grad
    upb[...] = jnp.broadcast_to(bias_sum, upb.shape)
    for step, out in enumerate(grad_ups):
        to = lax.rem(layer + step, layers)
        piece = total[pl.ds(pl.multiple_of(to * lanes, lanes), lanes), :] * scale
        out[...] = piece.astype(out.dtype)


def out_kernel(quads, layers, scale, act, down, *refs):
    cots, refs = refs[:quads], refs[quads:]
    grad_downs, refs = refs[:layers], refs[layers:]
    mixed, total = refs[:quads], refs[quads]
    layer, _ = place(quads)
    cells = cots[0].shape[0]
    part = down.shape[0] // layers
    for i in range(quads):
        block = act[i * cells : (i + 1) * cells, :]
        grad = lax.dot_general(
            block, cots[i][...], (((0,), (0,)), ((), ())), preferred_element_type=f32
        )
        total[...] = grad if i == 0 else total[...] + grad
    for step, out in enumerate(grad_downs):
        to = lax.rem(layer + step, layers)
        piece = total[pl.ds(pl.multiple_of(to * part, part), part), :] * scale
        out[...] = piece.astype(out.dtype)
    for i in range(quads):
        block = act[i * cells : (i + 1) * cells, :]
        mixed[i][...] = jnp.dot(block, down[...], preferred_element_type=f32).astype(
            mixed[i].dtype
        )


def norm_back_kernel(normed, inv, params, *refs):
    parts, (dconv, norms) = refs[:-2], refs[-2:]
    height, width, chans = dconv.shape
    gain_sum = jnp.zeros((1, chans), f32)
    shift_sum = jnp.zeros((1, chans), f32)
    for row in range(height):
        at = slice(row * width, (row + 1) * width)
        dnorm = parts[0][at, :].astype(f32)
        for part in parts[1:]:
            dnorm = dnorm + part[at, :].astype(f32)
        value = normed[at, :]
        gain_sum = gain_sum + jnp.sum(dnorm * value, axis=0, keepdims=True)
        shift_sum = shift_sum + jnp.sum(dnorm, axis=0, keepdims=True)
        scaled = dnorm * params[row_gain : row_gain + 1, 0:chans]
        mean = jnp.mean(scaled, axis=1, keepdims=True)
        cross = jnp.mean(scaled * value, axis=1, keepdims=True)
        dconv[row, :, :] = (inv[at, 0:1] * (scaled - mean - value * cross)).astype(bf16)
    norms[0:1, :] = gain_sum
    norms[1:2, :] = shift_sum


def up_split_kernel(quads, *refs):
    parts, outs = refs[:-quads], refs[-quads:]
    _, member = place(quads)
    own = outs[0].shape[0]
    total = parts[0]
    for other, out in enumerate(outs):
        row = pl.multiple_of(jnp.bitwise_xor(member, other) * own, own)
        piece = total[pl.ds(row, own), :].astype(f32)
        for part in parts[1:]:
            piece = piece + part[pl.ds(row, own), :].astype(f32)
        out[...] = piece


def up_join_kernel(quads, layers, *refs):
    pieces, out = refs[:-1], refs[-1]
    _, member = place(quads)
    part = out.shape[1] // (quads * layers)
    for s in range(quads):
        held = pieces[s][...]
        for m in range(1, quads):
            held = jnp.where(member == m, pieces[s ^ m][...], held)
        for z in range(layers):
            at = (z * quads + s) * part
            out[:, at : at + part] = held[:, z * part : (z + 1) * part]


def small_kernel(quads, part_up, *refs):
    parts, outs = refs[:-6], refs[-6:]
    _, member = place(quads)
    total = parts[0][...]
    for part in parts[1:]:
        total = total + part[...]
    own = outs[0].shape[1]
    down = lax.broadcasted_iota(jnp.int32, (lanes, own), 0)
    across = lax.broadcasted_iota(jnp.int32, (lanes, own), 1)
    pick = (down == across + member * own).astype(f32)
    mine = jnp.dot(total, pick, preferred_element_type=f32, precision=lax.Precision.HIGHEST)
    outs[0][...] = mine[0:taps, :]
    for row, out in zip((row_bias, row_gain, row_shift, row_down), outs[1:5]):
        out[...] = mine[row : row + 1, :]
    at = lax.broadcasted_iota(jnp.int32, total.shape, 0)
    chosen = jnp.where(at == row_up + member, total, 0.0)
    outs[5][...] = jnp.sum(chosen, axis=0, keepdims=True)[:, 0:part_up]


def per_device(
    features,
    cotangent,
    depth_weight,
    depth_bias,
    norm_gain,
    norm_shift,
    up_weight,
    up_bias,
    down_weight,
    down_bias,
):
    height, width, chans = features.shape
    devices = lax.axis_size("row")
    own, hidden_units = up_weight.shape
    part = down_weight.shape[0]
    layers = chans // lanes
    quads = devices // layers
    share = layers * part
    cells = height * width
    scale = 1.0 / math.sqrt(cells * devices)
    rows = round_up(row_up + quads, 16)
    pack_width = max(chans, share)

    def swap(value, other):
        return lax.ppermute(value, "row", [(i, i ^ other) for i in range(devices)])

    def turn(value, step):
        pairs = [
            (i, (i // quads + step) % layers * quads + i % quads) for i in range(devices)
        ]
        return lax.ppermute(value, "row", pairs)

    def around(value):
        return [value] + [turn(value, step) for step in range(1, layers)]

    def shift(value, step):
        pairs = [(i, i + step) for i in range(devices) if 0 <= i + step < devices]
        return lax.ppermute(value, "row", pairs)

    bits = []
    while 1 << len(bits) < quads:
        bits.append(1 << len(bits))

    def gather(value):
        held = {0: value}
        for bit in reversed(bits):
            held.update({i ^ bit: swap(block, bit) for i, block in list(held.items())})
        return [held[i] for i in range(quads)]

    def scatter(blocks):
        terms = []
        held = {i: [block] for i, block in enumerate(blocks)}
        for bit in bits:
            for i in [i for i in held if i & bit]:
                value = held.pop(i)
                value = functools.reduce(lambda a, b: a.astype(f32) + b.astype(f32), value)
                held[i ^ bit].append(swap(value.astype(bf16), bit))
        return held[0]

    downs = around(down_weight)
    shapes = [((rows + round_up(own, 16), pack_width), bf16)] * quads
    packs = call(
        functools.partial(pack_kernel, quads, layers, rows),
        shapes,
        (
            depth_weight,
            depth_bias.reshape(1, own),
            norm_gain.reshape(1, own),
            norm_shift.reshape(1, own),
            down_bias.reshape(1, own),
            up_bias.reshape(1, part),
            up_weight,
        ),
        [pltpu.VMEM((rows, own), f32)],
    )
    packs = [pack if i == 0 else swap(pack, i) for i, pack in enumerate(packs)]
    small, up = call(
        functools.partial(unpack_kernel, quads, rows, own),
        [((rows, pack_width), bf16), ((quads, own, share), bf16)],
        packs,
    )
    smalls = around(small)
    low, high = shift(features, 1), shift(features, -1)
    ups = around(up.reshape(quads * own, share))
    cots = gather(cotangent.reshape(cells, chans))

    rim = (height + 6, width + 16, chans)
    normal, normed, inv, params = call(
        conv_kernel,
        [
            ((cells, chans), bf16),
            ((cells, chans), f32),
            ((cells, lanes), f32),
            ((rows, pack_width), f32),
        ],
        (features, low, high, *smalls),
        [pltpu.VMEM(rim, f32), pltpu.VMEM((cells, chans), f32)],
        flops=20_000_000,
    )
    normals = gather(normal)

    outs = call(
        functools.partial(mlp_kernel, quads, layers, scale),
        [((lanes, share), f32)]
        + [((lanes, share), bf16)] * (layers - 1)
        + [((cells, chans), f32)]
        + [((cells, chans), bf16)] * (quads - 1)
        + [((quads * cells, share), bf16), ((8, share), f32), ((share, chans), bf16)],
        (params, *normals, *cots, *ups, *downs),
        [pltpu.VMEM((chans, share), bf16), pltpu.VMEM((chans, share), f32)],
        mib=40,
        flops=4_000_000_000,
    )
    grad_ups, dnorms = outs[:layers], outs[layers : layers + quads]
    act, upb, down_full = outs[layers + quads :]
    dnorms = scatter(dnorms)
    grad_ups = [grad_ups[0]] + [turn(grad_ups[i], i) for i in range(1, layers)]
    outs = call(
        functools.partial(out_kernel, quads, layers, scale),
        [((part, chans), f32)]
        + [((part, chans), bf16)] * (layers - 1)
        + [((cells, chans), f32)]
        + [((cells, chans), bf16)] * (quads - 1),
        (act, down_full, *cots),
        [pltpu.VMEM((share, chans), f32)],
        mib=40,
        flops=2_000_000_000,
    )
    grad_downs, mixed = outs[:layers], outs[layers:]
    grad_downs = [grad_downs[0]] + [turn(grad_downs[i], i) for i in range(1, layers)]
    mixed = scatter(mixed)

    dconv, norms = call(
        norm_back_kernel,
        [((height, width, chans), bf16), ((8, chans), f32)],
        (normed, inv, params, *dnorms),
    )
    low_back, high_back = shift(dconv, 1), shift(dconv, -1)
    grads = call(
        functools.partial(taps_kernel, quads, layers, scale),
        [((rows, lanes), f32)] * layers,
        (dconv, features, low, high, cotangent, norms, upb),
        [pltpu.VMEM(rim, f32), pltpu.VMEM((rows, chans), f32)],
        flops=20_000_000,
    )
    grads = [grads[0]] + [turn(grads[i], i) for i in range(1, layers)]
    total = functools.reduce(lambda a, b: a + b, grads)
    for bit in bits[:-1]:
        total = total + swap(total, bit)
    (grad_features,) = call(
        back_kernel,
        [((height, width, chans), bf16)],
        (dconv, low_back, high_back, cotangent, params),
        [pltpu.VMEM(rim, f32)],
        flops=20_000_000,
    )
    small_outs = call(
        functools.partial(small_kernel, quads, part),
        [((taps, own), f32)] + [((1, own), f32)] * 4 + [((1, part), f32)],
        (total, swap(total, bits[-1])),
    )
    grad_depth_weight = small_outs[0]
    grad_depth_bias, grad_norm_gain, grad_norm_shift, grad_down_bias, grad_up_bias = (
        value.reshape(-1) for value in small_outs[1:]
    )

    pieces = call(
        functools.partial(up_split_kernel, quads), [((own, share), f32)] * quads, grad_ups
    )
    pieces = [pieces[0]] + [swap(pieces[i], i) for i in range(1, quads)]
    (grad_up_weight,) = call(
        functools.partial(up_join_kernel, quads, layers), [((own, hidden_units), f32)], pieces
    )
    grad_down_weight = functools.reduce(lambda a, b: a + b.astype(f32), grad_downs)
    mixed = functools.reduce(lambda a, b: a.astype(f32) + b.astype(f32), mixed)
    block_out = (
        features.astype(f32)
        + (mixed + params[row_down, 0:chans]).reshape(height, width, chans)
    ).astype(bf16)
    return (
        block_out,
        grad_features,
        grad_up_weight,
        grad_down_weight,
        grad_depth_weight,
        grad_depth_bias,
        grad_norm_gain,
        grad_norm_shift,
        grad_up_bias,
        grad_down_bias,
    )


def solution(mesh):
    placed = (
        P(("groups", "row"), None, None),
        P(("groups", "row"), None, None),
        P(None, "row"),
        P("row"),
        P("row"),
        P("row"),
        P("row", None),
        P("row"),
        P("row", None),
        P("row"),
    )
    return jax.shard_map(
        per_device,
        mesh=mesh,
        in_specs=placed,
        out_specs=(
            P(("groups", "row"), None, None),
            P(("groups", "row"), None, None),
            P(("groups", "row"), None),
            P(("groups", "row"), None),
            P("groups", "row"),
            P(("groups", "row")),
            P(("groups", "row")),
            P(("groups", "row")),
            P(("groups", "row")),
            P(("groups", "row")),
        ),
        check_vma=False,
    )
```

```python
import functools
import math

import jax
import jax.numpy as jnp
from jax import lax
from jax.experimental import pallas as pl
from jax.experimental.pallas import tpu as pltpu
from jax.sharding import PartitionSpec as P

eps = 1e-06
lanes = 128
taps = 49
f32 = jnp.float32
bf16 = jnp.bfloat16
row_bias, row_gain, row_shift, row_down, row_up = 49, 50, 51, 52, 53


def round_up(value, unit):
    return (value + unit - 1) // unit * unit


def call(kernel, outs, args, scratch=(), mib=24, flops=1000, moved=1000, space=pltpu.VMEM):
    return pl.pallas_call(
        kernel,
        out_shape=[jax.ShapeDtypeStruct(shape, dtype) for shape, dtype in outs],
        in_specs=[pl.BlockSpec(memory_space=space)] * len(args),
        out_specs=[pl.BlockSpec(memory_space=pltpu.VMEM)] * len(outs),
        scratch_shapes=list(scratch),
        compiler_params=pltpu.CompilerParams(vmem_limit_bytes=mib * 1024 * 1024),
        cost_estimate=pl.CostEstimate(flops=flops, bytes_accessed=moved, transcendentals=0),
    )(*args)


def place(quads):
    index = lax.axis_index("row")
    return index // quads, lax.rem(index, quads)


def one_hot(rows, columns, offset):
    down = lax.broadcasted_iota(jnp.int32, (rows, columns), 0)
    across = lax.broadcasted_iota(jnp.int32, (rows, columns), 1)
    return (across == down + offset).astype(f32)


def pack_kernel(quads, layers, rows, *refs):
    given, refs = refs[:7], refs[7:]
    near, small, far, (held, head, *local), sems = (
        refs[: quads // 2],
        refs[quads // 2],
        refs[quads // 2 + 1],
        refs[quads // 2 + 2 : -1],
        refs[-1],
    )
    copies = [
        pltpu.make_async_copy(source, target, sems.at[i])
        for i, (source, target) in enumerate(zip(given, local))
    ]
    for copy in copies:
        copy.start()
    for copy in copies:
        copy.wait()
    dw, db, gain, shift, down, upb, up = local
    _, member = place(quads)
    own = dw.shape[0]
    part = upb.shape[1]
    step = round_up(own, 16)
    spread = one_hot(own, lanes, member * own).astype(bf16)
    held[...] = jnp.zeros_like(held)
    held[row_bias : row_bias + 1, :] = db[...].astype(f32)
    held[row_gain : row_gain + 1, :] = gain[...].astype(f32)
    held[row_shift : row_shift + 1, :] = shift[...].astype(f32)
    held[row_down : row_down + 1, :] = down[...].astype(f32)
    head[...] = jnp.dot(held[...].astype(bf16), spread, preferred_element_type=f32)
    head[0:taps, :] = lax.dot_general(
        dw[...], spread, (((0,), (0,)), ((), ())), preferred_element_type=f32
    )
    for s in range(quads):
        head[row_up + s : row_up + s + 1, 0:part] = jnp.where(
            member == s, upb[...].astype(f32), 0.0
        )
    small[...] = head[...].astype(bf16)
    far[0:rows, :] = head[...].astype(bf16)
    wide = [up[:, i * part : (i + 1) * part] for i in range(layers * quads)]
    for other in range(quads):
        partner = jnp.bitwise_xor(member, other)
        if other < quads // 2:
            out, base = near[other], 0
        else:
            out, base = far, rows + (other - quads // 2) * layers * step
        if step != own or part != lanes:
            out[base : base + layers * step, :] = jnp.zeros((layers * step, lanes), bf16)
        for z in range(layers):
            piece = wide[z * quads]
            for s in range(1, quads):
                piece = jnp.where(partner == s, wide[z * quads + s], piece)
            out[base + z * step : base + z * step + own, 0:part] = piece


def unpack_kernel(quads, layers, down, *refs):
    pieces, out = refs[:-1], refs[-1]
    _, member = place(quads)
    blocks, own, share = out.shape
    ahead = blocks - quads
    part = share // layers
    step = round_up(own, 16)
    for i in range(ahead):
        out[i] = down[i * own : (i + 1) * own, :]
    for other, piece in enumerate(pieces):
        to = ahead + jnp.bitwise_xor(member, other)
        for z in range(layers):
            block = piece[z * step : (z + 1) * step, :]
            out[to, :, z * part : (z + 1) * part] = block[0:own, 0:part]


def fill(padded, block, outer, inner, width):
    height = block.shape[0]
    even = lax.rem(lax.axis_index("row"), 2) == 0
    rows, columns, chans = padded.shape
    zero = jnp.zeros((rows, 8, chans), f32)
    padded[:, 0:8, :] = zero
    padded[:, 8 + width :, :] = jnp.zeros((rows, columns - 8 - width, chans), f32)
    low = jnp.where(even, outer[height - 3 :, :, :], inner[height - 3 :, :, :])
    high = jnp.where(even, inner[0:3, :, :], outer[0:3, :, :])
    padded[0:3, 8 : 8 + width, :] = low.astype(f32)
    padded[3 : 3 + height, 8 : 8 + width, :] = block[...].astype(f32)
    padded[3 + height :, 8 : 8 + width, :] = high.astype(f32)


def slide(padded, weights, height, width, at, flip):
    tiles = (width // 8, 8, lanes)
    sums = [jnp.zeros(tiles, f32) for _ in range(height)]
    for second in range(7):
        order = [first * 7 + second for first in range(7)]
        order = [taps - 1 - tap if flip else tap for tap in order]
        held = [jnp.broadcast_to(weights[tap : tap + 1, at], tiles[1:]) for tap in order]
        for row in range(height + 6):
            piece = padded[row, 5 + second : 5 + second + width, at].reshape(tiles)
            for out in range(height):
                if 0 <= row - out < 7:
                    sums[out] = sums[out] + piece * held[row - out]
    return [value.reshape(width, lanes) for value in sums]


def conv_kernel(quads, layers, features, outer, inner, *refs):
    smalls, (normal, normed, inv, params, bias, padded, conv) = refs[:-7], refs[-7:]
    height, width, chans = features.shape
    layer, member = place(quads)
    for other, small in enumerate(smalls):
        at = pl.multiple_of(jnp.bitwise_xor(layer, other) * lanes, lanes)
        params[:, pl.ds(at, lanes)] = small[...].astype(f32)
    part = bias.shape[1] // layers
    for z in range(layers):
        at = slice(z * lanes, z * lanes + part)
        value = params[row_up : row_up + 1, at]
        for s in range(1, quads):
            value = jnp.where(member == s, params[row_up + s : row_up + s + 1, at], value)
        bias[:, z * part : (z + 1) * part] = jnp.broadcast_to(value, (8, part))
    fill(padded, features, outer, inner, width)

    def chunk(i, carry):
        at = pl.ds(pl.multiple_of(i * lanes, lanes), lanes)
        sums = slide(padded, params, height, width, at, False)
        for out in range(height):
            conv[out * width : (out + 1) * width, at] = (
                sums[out] + params[row_bias : row_bias + 1, at]
            )
        return carry

    lax.fori_loop(0, chans // lanes, chunk, 0)

    def norm(i, carry):
        at = pl.ds(pl.multiple_of(i * width, width), width)
        value = conv[at, :]
        centered = value - jnp.mean(value, axis=1, keepdims=True)
        var = jnp.mean(centered * centered, axis=1, keepdims=True)
        scale = lax.rsqrt(var + eps)
        value = centered * scale
        normed[at, :] = value
        inv[at, :] = jnp.broadcast_to(scale, (width, lanes))
        normal[at, :] = (
            value * params[row_gain : row_gain + 1, 0:chans]
            + params[row_shift : row_shift + 1, 0:chans]
        ).astype(bf16)
        return carry

    lax.fori_loop(0, height, norm, 0)


def back_kernel(dconv, outer, inner, cotangent, params, out, padded):
    height, width, chans = dconv.shape
    fill(padded, dconv, outer, inner, width)

    def chunk(i, carry):
        at = pl.ds(pl.multiple_of(i * lanes, lanes), lanes)
        sums = slide(padded, params, height, width, at, True)
        for row in range(height):
            out[row, :, at] = (cotangent[row, :, at].astype(f32) + sums[row]).astype(bf16)
        return carry

    lax.fori_loop(0, chans // lanes, chunk, 0)


def taps_kernel(
    quads, layers, scale, dconv, features, outer, inner, cotangent, norms, upb, *refs
):
    kept, sent, padded, grads = refs
    height, width, chans = dconv.shape
    layer, member = place(quads)
    fill(padded, features, outer, inner, width)
    grads[...] = jnp.zeros_like(grads)

    def fold(value):
        return jnp.sum(value.reshape(width // 8, 8, lanes), axis=0)

    def chunk(i, carry):
        at = pl.ds(pl.multiple_of(i * lanes, lanes), lanes)
        own = [dconv[row, :, at].astype(f32) for row in range(height)]
        for second in range(7):
            sums = [jnp.zeros((8, lanes), f32) for _ in range(7)]
            for row in range(height + 6):
                piece = padded[row, 5 + second : 5 + second + width, at]
                for out in range(height):
                    first = row - out
                    if 0 <= first < 7:
                        sums[first] = sums[first] + fold(own[out] * piece)
            for first in range(7):
                tap = first * 7 + second
                grads[tap : tap + 1, at] = (
                    jnp.sum(sums[first], axis=0, keepdims=True) * scale
                )
        total = fold(own[0])
        for row in range(1, height):
            total = total + fold(own[row])
        grads[row_bias : row_bias + 1, at] = jnp.sum(total, axis=0, keepdims=True) * scale
        total = fold(cotangent[0, :, at].astype(f32))
        for row in range(1, height):
            total = total + fold(cotangent[row, :, at].astype(f32))
        grads[row_down : row_down + 1, at] = jnp.sum(total, axis=0, keepdims=True) * scale
        grads[row_gain : row_gain + 1, at] = norms[0:1, at] * scale
        grads[row_shift : row_shift + 1, at] = norms[1:2, at] * scale
        return carry

    lax.fori_loop(0, chans // lanes, chunk, 0)
    part = upb.shape[1] // layers
    for z in range(layers):
        bias = upb[0:1, z * part : (z + 1) * part] * scale
        for s in range(quads):
            grads[row_up + s : row_up + s + 1, z * lanes : z * lanes + part] = jnp.where(
                member == s, bias, 0.0
            )
    for other in range(layers):
        at = pl.multiple_of(jnp.bitwise_xor(layer, other) * lanes, lanes)
        out, i = (kept, other) if other < layers // 2 else (sent, other - layers // 2)
        out[i] = grads[:, pl.ds(at, lanes)]


def mlp_kernel(quads, layers, bias_row, *refs):
    normals, refs = refs[:quads], refs[quads:]
    cots, refs = refs[:quads], refs[quads:]
    weights, (total, even, odd, act, upb, down, up) = refs[:-7], refs[-7:]
    layer, _ = place(quads)
    cells, chans = normals[0].shape
    hidden_units = act.shape[1]
    part = hidden_units // layers
    for step in range(layers):
        source = lax.rem(layer - step + layers, layers)
        if len(weights) == layers:
            one, two = weights[step].at[0:part], weights[step].at[part:]
        else:
            one, two = weights[step], weights[layers + step]
        down[pl.ds(pl.multiple_of(source * part, part), part), :] = one[...]
        up[pl.ds(pl.multiple_of(source * lanes, lanes), lanes), :] = two[...]
    bias = bias_row[0:1, :]
    bias_sum = jnp.zeros((1, hidden_units), f32)
    for i in range(quads):
        hidden = jnp.dot(normals[i][...], up[...], preferred_element_type=f32) + bias
        dact = lax.dot_general(
            cots[i][...], down[...], (((1,), (1,)), ((), ())), preferred_element_type=f32
        )
        cumulative = 0.5 * (1.0 + lax.erf(hidden * (1.0 / math.sqrt(2.0))))
        density = jnp.exp(-0.5 * hidden * hidden) * (1.0 / math.sqrt(2.0 * math.pi))
        act[i * cells : (i + 1) * cells, :] = (hidden * cumulative).astype(bf16)
        dhidden = (dact * (cumulative + hidden * density)).astype(bf16)
        bias_sum = bias_sum + jnp.sum(dhidden.astype(f32), axis=0, keepdims=True)
        dnorm = lax.dot_general(
            dhidden, up[...], (((1,), (1,)), ((), ())), preferred_element_type=f32
        )
        at = slice(i // 2 * cells, (i // 2 + 1) * cells)
        if i % 2:
            odd[at, :] = dnorm.astype(bf16)
        else:
            even[at, :] = dnorm
        grad = lax.dot_general(
            normals[i][...], dhidden, (((0,), (0,)), ((), ())), preferred_element_type=f32
        )
        total[...] = grad if i == 0 else total[...] + grad
    upb[...] = jnp.broadcast_to(bias_sum, upb.shape)


def out_kernel(quads, layers, scale, total_up, act, down, *refs):
    cots, refs = refs[:quads], refs[quads:]
    own_down, own_up, refs = refs[0], refs[1], refs[2:]
    sends, (even, odd, total) = refs[:-3], refs[-3:]
    layer, _ = place(quads)
    cells = cots[0].shape[0]
    part = down.shape[0] // layers
    for i in range(quads):
        block = act[i * cells : (i + 1) * cells, :]
        grad = lax.dot_general(
            block, cots[i][...], (((0,), (0,)), ((), ())), preferred_element_type=f32
        )
        total[...] = grad if i == 0 else total[...] + grad
    for step in range(layers):
        if step == 0:
            one, two = own_down, own_up
        elif len(sends) == layers - 1:
            one, two = sends[step - 1].at[0:part], sends[step - 1].at[part:]
        else:
            one, two = sends[step - 1], sends[layers - 2 + step]
        to = lax.rem(layer + step, layers)
        piece = total[pl.ds(pl.multiple_of(to * part, part), part), :] * scale
        one[...] = piece.astype(one.dtype)
        piece = total_up[pl.ds(pl.multiple_of(to * lanes, lanes), lanes), :] * scale
        two[...] = piece.astype(two.dtype)
    for i in range(quads):
        block = act[i * cells : (i + 1) * cells, :]
        mixed = jnp.dot(block, down[...], preferred_element_type=f32)
        at = slice(i // 2 * cells, (i // 2 + 1) * cells)
        if i % 2:
            odd[at, :] = mixed.astype(bf16)
        else:
            even[at, :] = mixed


def norm_back_kernel(normed, inv, params, *refs):
    parts, (dconv, norms) = refs[:-2], refs[-2:]
    height, width, chans = dconv.shape
    gain_sum = jnp.zeros((1, chans), f32)
    shift_sum = jnp.zeros((1, chans), f32)
    for row in range(height):
        at = slice(row * width, (row + 1) * width)
        dnorm = parts[0][at, :].astype(f32)
        for part in parts[1:]:
            dnorm = dnorm + part[at, :].astype(f32)
        value = normed[at, :]
        gain_sum = gain_sum + jnp.sum(dnorm * value, axis=0, keepdims=True)
        shift_sum = shift_sum + jnp.sum(dnorm, axis=0, keepdims=True)
        scaled = dnorm * params[row_gain : row_gain + 1, 0:chans]
        mean = jnp.mean(scaled, axis=1, keepdims=True)
        cross = jnp.mean(scaled * value, axis=1, keepdims=True)
        dconv[row, :, :] = (inv[at, 0:1] * (scaled - mean - value * cross)).astype(bf16)
    norms[0:1, :] = gain_sum
    norms[1:2, :] = shift_sum


def up_split_kernel(quads, part, *refs):
    own_down, own_up, refs = refs[0], refs[1], refs[2:]
    terms, out_down, outs = refs[: -quads - 1], refs[-quads - 1], refs[-quads:]
    _, member = place(quads)
    if terms[0].shape[0] > lanes:
        downs = [term.at[0:part] for term in terms]
        ups = [term.at[part:] for term in terms]
    else:
        downs, ups = terms[: len(terms) // 2], terms[len(terms) // 2 :]
    total = own_down[...]
    for term in downs:
        total = total + term[...].astype(f32)
    out_down[...] = total
    own = outs[0].shape[0]
    for other, out in enumerate(outs):
        row = pl.multiple_of(jnp.bitwise_xor(member, other) * own, own)
        piece = own_up[pl.ds(row, own), :]
        for term in ups:
            piece = piece + term[pl.ds(row, own), :].astype(f32)
        out[...] = piece.astype(out.dtype)


def up_join_kernel(quads, layers, *refs):
    pieces, out = refs[:-1], refs[-1]
    _, member = place(quads)
    part = out.shape[1] // (quads * layers)
    for s in range(quads):
        held = pieces[s][...].astype(f32)
        for m in range(1, quads):
            held = jnp.where(member == m, pieces[s ^ m][...].astype(f32), held)
        for z in range(layers):
            at = (z * quads + s) * part
            out[:, at : at + part] = held[:, z * part : (z + 1) * part]


def small_kernel(quads, part_up, *refs):
    parts, outs = refs[:-6], refs[-6:]
    _, member = place(quads)
    total = parts[0][...]
    for part in parts[1:]:
        total = total + part[...]
    own = outs[0].shape[0]
    down = lax.broadcasted_iota(jnp.int32, (lanes, own), 0)
    across = lax.broadcasted_iota(jnp.int32, (lanes, own), 1)
    pick = (down == across + member * own).astype(f32)
    mine = jnp.dot(total, pick, preferred_element_type=f32, precision=lax.Precision.HIGHEST)
    outs[0][...] = lax.dot_general(
        pick,
        total[0:taps, :],
        (((0,), (1,)), ((), ())),
        preferred_element_type=f32,
        precision=lax.Precision.HIGHEST,
    )
    for row, out in zip((row_bias, row_gain, row_shift, row_down), outs[1:5]):
        out[...] = mine[row : row + 1, :]
    at = lax.broadcasted_iota(jnp.int32, total.shape, 0)
    chosen = jnp.where(at == row_up + member, total, 0.0)
    outs[5][...] = jnp.sum(chosen, axis=0, keepdims=True)[:, 0:part_up]


def per_device(
    features,
    cotangent,
    depth_weight,
    depth_bias,
    norm_gain,
    norm_shift,
    up_weight,
    up_bias,
    down_weight,
    down_bias,
):
    height, width, chans = features.shape
    devices = lax.axis_size("row")
    own, hidden_units = up_weight.shape
    part = down_weight.shape[0]
    layers = chans // lanes
    quads = devices // layers
    share = layers * part
    cells = height * width
    scale = 1.0 / math.sqrt(cells * devices)
    rows = round_up(row_up + quads, 16)

    def swap(value, other):
        return lax.ppermute(value, "row", [(i, i ^ other) for i in range(devices)])

    def turn(value, step=1):
        pairs = [
            (i, (i // quads + step) % layers * quads + i % quads) for i in range(devices)
        ]
        return lax.ppermute(value, "row", pairs)

    def halo(value):
        pairs = [(i, i + 1) for i in range(1, devices - 1, 2)]
        pairs = pairs + [(target, source) for source, target in pairs]
        return lax.ppermute(value, "row", pairs), swap(value, 1)

    def cross(value, other):
        return lax.ppermute(
            value, "row", [(i, (i // quads ^ other) * quads + i % quads) for i in range(devices)]
        )

    def add(one, two, kind):
        return (one.astype(f32) + two.astype(f32)).astype(kind)

    bits = []
    while 1 << len(bits) < quads:
        bits.append(1 << len(bits))

    def exchange(pieces, bit, extra=None):
        keys = sorted(key for key in pieces if key[0] & bit)
        blocks = [pieces[key] for key in keys]
        ahead, size = 0, blocks[0].shape[0]
        if extra is not None and extra.shape[1] == blocks[0].shape[1]:
            ahead = extra.shape[0]
            got = swap(jnp.concatenate([extra] + blocks, axis=0), bit)
            extra = got[:ahead]
        else:
            got = swap(jnp.concatenate(blocks, axis=0), bit)
            extra = None if extra is None else swap(extra, bit)
        kept = {key: piece for key, piece in pieces.items() if not key[0] & bit}
        for i, (target, source) in enumerate(keys):
            at = ahead + i * size
            kept[target ^ bit, source ^ bit] = got[at : at + size]
        return kept, extra

    def spread(held, bits):
        for bit in reversed(bits):
            held.update({i ^ bit: swap(block, bit) for i, block in list(held.items())})

    def near(even, odd):
        return even, swap(odd, bits[0])

    def far(even, odd):
        held = add(even, odd, f32).reshape(-1, cells, chans)
        for bit in bits[1:-1]:
            pairs = held.reshape(-1, 2, cells, chans)
            held = pairs[:, 0] + swap(pairs[:, 1].astype(bf16), bit).astype(f32)
        return held[0], held[1].astype(bf16)

    step = round_up(own, 16)
    block = layers * step
    *pieces, small, far_pack = call(
        functools.partial(pack_kernel, quads, layers, rows),
        [((block, lanes), bf16)] * (quads // 2)
        + [((rows, lanes), bf16), ((rows + quads // 2 * block, lanes), bf16)],
        (
            depth_weight.T,
            depth_bias.reshape(1, own),
            norm_gain.reshape(1, own),
            norm_shift.reshape(1, own),
            down_bias.reshape(1, own),
            up_bias.reshape(1, part),
            up_weight,
        ),
        [pltpu.VMEM((rows, own), f32), pltpu.VMEM((rows, lanes), f32)]
        + [pltpu.VMEM((own, taps), bf16)]
        + [pltpu.VMEM((1, own), bf16)] * 4
        + [pltpu.VMEM((1, part), bf16), pltpu.VMEM((own, hidden_units), bf16)]
        + [pltpu.SemaphoreType.DMA((7,))],
        space=pl.ANY,
        mib=60,
    )
    features, cotangent, down_weight = lax.optimization_barrier(
        (features, cotangent, down_weight, small)
    )[:3]
    got = swap(far_pack, bits[-1])
    pieces = {(i, 0): piece for i, piece in enumerate(pieces)}
    for i in range(quads // 2):
        pieces[i, bits[-1]] = got[rows + i * block : rows + (i + 1) * block]
    small = small + got[:rows]
    small, pieces = lax.optimization_barrier((small, pieces))
    for bit in reversed(bits[:-1]):
        pieces, got = exchange(pieces, bit, small)
        small = small + got
    small, pieces = lax.optimization_barrier((small, pieces))
    merged = share == chans and own % 16 == 0 and part % own == 0
    (up,) = call(
        functools.partial(unpack_kernel, quads, layers),
        [(((part // own if merged else 0) + quads, own, share), bf16)],
        [down_weight] + [pieces[0, i] for i in range(quads)],
    )
    up = up.reshape(-1, share)
    weights = [[up]] if merged else [[down_weight], [up]]
    for held in weights:
        held.extend(turn(held[0], step) for step in range(1, layers))
    outer, inner = halo(features)
    cots = {0: cotangent.reshape(cells, chans)}
    spread(cots, bits[1:])
    smalls = small
    other = 1
    while other < layers:
        smalls = jnp.concatenate([smalls, cross(smalls, other)], axis=0)
        other *= 2
    first = [held[1] for held in weights]
    smalls, first = lax.optimization_barrier((smalls, first))
    for held, value in zip(weights, first):
        held[1] = value
    smalls = [smalls[i * rows : (i + 1) * rows] for i in range(layers)]

    rim = (height + 6, width + 16, chans)
    normal, normed, inv, params, bias = call(
        functools.partial(conv_kernel, quads, layers),
        [
            ((cells, chans), bf16),
            ((cells, chans), f32),
            ((cells, lanes), f32),
            ((rows, chans), f32),
            ((8, share), f32),
        ],
        (features, outer, inner, *smalls),
        [pltpu.VMEM(rim, f32), pltpu.VMEM((cells, chans), f32)],
    )
    first = [held[-1] for held in weights]
    normal, cots, first = lax.optimization_barrier((normal, cots, first))
    for held, value in zip(weights, first):
        held[-1] = value
    normals = {0: normal}
    spread(normals, bits[1:])
    normals, weights = lax.optimization_barrier((normals, weights))
    spread(cots, bits[:1])
    spread(normals, bits[:1])
    normals, cots = ([held[i] for i in range(quads)] for held in (normals, cots))

    half = quads // 2 * cells
    total_up, even, odd, act, upb, down_full = call(
        functools.partial(mlp_kernel, quads, layers),
        [((chans, share), f32), ((half, chans), f32), ((half, chans), bf16)]
        + [((quads * cells, share), bf16), ((8, share), f32), ((share, chans), bf16)],
        (bias, *normals, *cots, *(block for held in weights for block in held)),
        [pltpu.VMEM((chans, share), bf16)],
        mib=40,
    )
    sums = near(even, odd)
    if merged:
        shapes = [(part + lanes, chans)] * (layers - 1)
    else:
        shapes = [(part, chans)] * (layers - 1) + [(lanes, share)] * (layers - 1)
    own_down, own_up, *sends, even, odd = call(
        functools.partial(out_kernel, quads, layers, scale),
        [((part, chans), f32), ((lanes, share), f32)]
        + [(shape, bf16) for shape in shapes]
        + [((half, chans), f32), ((half, chans), bf16)],
        (total_up, act, down_full, *cots),
        [pltpu.VMEM((share, chans), f32)],
        mib=40,
    )
    sums, sends = lax.optimization_barrier((sums, sends))
    kept, sent = far(*sums)
    dnorms = [kept, swap(sent, bits[-1])]
    terms = [turn(send, i % (layers - 1) + 1) for i, send in enumerate(sends)]
    dnorms, even, odd, terms[0] = lax.optimization_barrier((dnorms, even, odd, terms[0]))

    dconv, norms = call(
        norm_back_kernel,
        [((height, width, chans), bf16), ((8, chans), f32)],
        (normed, inv, params, *dnorms),
    )
    even, odd = lax.optimization_barrier((even, odd, dconv))[:2]
    outer_back, inner_back = halo(dconv)
    sums = near(even, odd)
    kept, sent = call(
        functools.partial(taps_kernel, quads, layers, scale),
        [((layers // 2, rows, lanes), f32)] * 2,
        (dconv, features, outer, inner, cotangent, norms, upb),
        [pltpu.VMEM(rim, f32), pltpu.VMEM((rows, chans), f32)],
    )
    mixed, across = far(*sums)
    across = swap(across, bits[-1])
    kept, sent, terms[2:] = lax.optimization_barrier((kept, sent, terms[2:]))
    total = kept + cross(sent, layers // 2)
    total, outer_back, inner_back, terms, across = lax.optimization_barrier(
        (total, outer_back, inner_back, terms, across)
    )
    while total.shape[0] > 1:
        middle = total.shape[0] // 2
        total = total[:middle] + cross(total[middle:], middle)
    total = total[0]
    grad_down_weight, *pieces = call(
        functools.partial(up_split_kernel, quads, part),
        [((part, chans), f32), ((own, share), f32)] + [((own, share), bf16)] * (quads - 1),
        (own_down, own_up, *terms),
    )
    pieces = {(i, 0): piece for i, piece in enumerate(pieces)}
    pieces, _ = exchange(pieces, bits[-1])
    for bit in bits[:-1]:
        total = total + swap(total, bit)
    total, outer_back, inner_back, across = lax.optimization_barrier(
        (total, outer_back, inner_back, across)
    )
    last = swap(total, bits[-1])
    (grad_features,) = call(
        back_kernel,
        [((height, width, chans), bf16)],
        (dconv, outer_back, inner_back, cotangent, params),
        [pltpu.VMEM(rim, f32)],
    )
    for bit in reversed(bits[:-1]):
        pieces, _ = exchange(pieces, bit)
    small_outs = call(
        functools.partial(small_kernel, quads, part),
        [((own, taps), f32)] + [((1, own), f32)] * 4 + [((1, part), f32)],
        (total, last),
    )
    grad_depth_weight = small_outs[0].T
    grad_depth_bias, grad_norm_gain, grad_norm_shift, grad_down_bias, grad_up_bias = (
        value.reshape(-1) for value in small_outs[1:]
    )

    (grad_up_weight,) = call(
        functools.partial(up_join_kernel, quads, layers),
        [((own, hidden_units), f32)],
        [pieces[0, i] for i in range(quads)],
    )
    mixed = mixed + across.astype(f32)
    block_out = (
        features.astype(f32)
        + (mixed + params[row_down, 0:chans]).reshape(height, width, chans)
    ).astype(bf16)
    return (
        block_out,
        grad_features,
        grad_up_weight,
        grad_down_weight,
        grad_depth_weight,
        grad_depth_bias,
        grad_norm_gain,
        grad_norm_shift,
        grad_up_bias,
        grad_down_bias,
    )


def solution(mesh):
    placed = (
        P(("groups", "row"), None, None),
        P(("groups", "row"), None, None),
        P(None, "row"),
        P("row"),
        P("row"),
        P("row"),
        P("row", None),
        P("row"),
        P("row", None),
        P("row"),
    )
    return jax.shard_map(
        per_device,
        mesh=mesh,
        in_specs=placed,
        out_specs=(
            P(("groups", "row"), None, None),
            P(("groups", "row"), None, None),
            P(("groups", "row"), None),
            P(("groups", "row"), None),
            P("groups", "row"),
            P(("groups", "row")),
            P(("groups", "row")),
            P(("groups", "row")),
            P(("groups", "row")),
            P(("groups", "row")),
        ),
        check_vma=False,
    )
```

```python
import functools
import math

import jax
import jax.numpy as jnp
from jax import lax
from jax.experimental import pallas as pl
from jax.experimental.pallas import tpu as pltpu
from jax.sharding import PartitionSpec as P

eps = 1e-06
lanes = 128
taps = 49
f32 = jnp.float32
bf16 = jnp.bfloat16
row_bias, row_gain, row_shift, row_down, row_up = 49, 50, 51, 52, 53


def round_up(value, unit):
    return (value + unit - 1) // unit * unit


def call(kernel, outs, args, scratch=(), mib=24, flops=1000, moved=1000, space=pltpu.VMEM):
    return pl.pallas_call(
        kernel,
        out_shape=[jax.ShapeDtypeStruct(shape, dtype) for shape, dtype in outs],
        in_specs=[pl.BlockSpec(memory_space=space)] * len(args),
        out_specs=[pl.BlockSpec(memory_space=pltpu.VMEM)] * len(outs),
        scratch_shapes=list(scratch),
        compiler_params=pltpu.CompilerParams(vmem_limit_bytes=mib * 1024 * 1024),
        cost_estimate=pl.CostEstimate(flops=flops, bytes_accessed=moved, transcendentals=0),
    )(*args)


def place(quads):
    index = lax.axis_index("row")
    return index // quads, lax.rem(index, quads)


def one_hot(rows, columns, offset):
    down = lax.broadcasted_iota(jnp.int32, (rows, columns), 0)
    across = lax.broadcasted_iota(jnp.int32, (rows, columns), 1)
    return (across == down + offset).astype(f32)


def pack_kernel(quads, layers, rows, *refs):
    given, refs = refs[:7], refs[7:]
    near, small, far, (held, head, *local), sems = (
        refs[: quads // 2],
        refs[quads // 2],
        refs[quads // 2 + 1],
        refs[quads // 2 + 2 : -1],
        refs[-1],
    )
    copies = [
        pltpu.make_async_copy(source, target, sems.at[i])
        for i, (source, target) in enumerate(zip(given, local))
    ]
    for copy in copies:
        copy.start()
    for copy in copies:
        copy.wait()
    dw, db, gain, shift, down, upb, up = local
    _, member = place(quads)
    own = dw.shape[0]
    part = upb.shape[1]
    step = round_up(own, 16)
    spread = one_hot(own, lanes, member * own).astype(bf16)
    held[...] = jnp.zeros_like(held)
    held[row_bias : row_bias + 1, :] = db[...].astype(f32)
    held[row_gain : row_gain + 1, :] = gain[...].astype(f32)
    held[row_shift : row_shift + 1, :] = shift[...].astype(f32)
    held[row_down : row_down + 1, :] = down[...].astype(f32)
    head[...] = jnp.dot(held[...].astype(bf16), spread, preferred_element_type=f32)
    head[0:taps, :] = lax.dot_general(
        dw[...], spread, (((0,), (0,)), ((), ())), preferred_element_type=f32
    )
    for s in range(quads):
        head[row_up + s : row_up + s + 1, 0:part] = jnp.where(
            member == s, upb[...].astype(f32), 0.0
        )
    small[...] = head[...].astype(bf16)
    far[0:rows, :] = head[...].astype(bf16)
    wide = [up[:, i * part : (i + 1) * part] for i in range(layers * quads)]
    for other in range(quads):
        partner = jnp.bitwise_xor(member, other)
        if other < quads // 2:
            out, base = near[other], 0
        else:
            out, base = far, rows + (other - quads // 2) * layers * step
        if step != own or part != lanes:
            out[base : base + layers * step, :] = jnp.zeros((layers * step, lanes), bf16)
        for z in range(layers):
            piece = wide[z * quads]
            for s in range(1, quads):
                piece = jnp.where(partner == s, wide[z * quads + s], piece)
            out[base + z * step : base + z * step + own, 0:part] = piece


def unpack_kernel(quads, layers, down, *refs):
    pieces, out = refs[:-1], refs[-1]
    _, member = place(quads)
    blocks, own, share = out.shape
    ahead = blocks - quads
    part = share // layers
    step = round_up(own, 16)
    for i in range(ahead):
        out[i] = down[i * own : (i + 1) * own, :]
    for other, piece in enumerate(pieces):
        to = ahead + jnp.bitwise_xor(member, other)
        for z in range(layers):
            block = piece[z * step : (z + 1) * step, :]
            out[to, :, z * part : (z + 1) * part] = block[0:own, 0:part]


def fill(padded, block, outer, inner, width):
    height = block.shape[0]
    even = lax.rem(lax.axis_index("row"), 2) == 0
    rows, columns, chans = padded.shape
    zero = jnp.zeros((rows, 8, chans), f32)
    padded[:, 0:8, :] = zero
    padded[:, 8 + width :, :] = jnp.zeros((rows, columns - 8 - width, chans), f32)
    low = jnp.where(even, outer[height - 3 :, :, :], inner[height - 3 :, :, :])
    high = jnp.where(even, inner[0:3, :, :], outer[0:3, :, :])
    padded[0:3, 8 : 8 + width, :] = low.astype(f32)
    padded[3 : 3 + height, 8 : 8 + width, :] = block[...].astype(f32)
    padded[3 + height :, 8 : 8 + width, :] = high.astype(f32)


def slide(padded, weights, height, width, at, flip):
    tiles = (width // 8, 8, lanes)
    sums = [jnp.zeros(tiles, f32) for _ in range(height)]
    for second in range(7):
        order = [first * 7 + second for first in range(7)]
        order = [taps - 1 - tap if flip else tap for tap in order]
        held = [jnp.broadcast_to(weights[tap : tap + 1, at], tiles[1:]) for tap in order]
        for row in range(height + 6):
            piece = padded[row, 5 + second : 5 + second + width, at].reshape(tiles)
            for out in range(height):
                if 0 <= row - out < 7:
                    sums[out] = sums[out] + piece * held[row - out]
    return [value.reshape(width, lanes) for value in sums]


def conv_kernel(quads, layers, features, outer, inner, *refs):
    smalls, (normal, normed, inv, params, bias, padded, conv) = refs[:-7], refs[-7:]
    height, width, chans = features.shape
    layer, member = place(quads)
    for other, small in enumerate(smalls):
        at = pl.multiple_of(jnp.bitwise_xor(layer, other) * lanes, lanes)
        params[:, pl.ds(at, lanes)] = small[...].astype(f32)
    part = bias.shape[1] // layers
    for z in range(layers):
        at = slice(z * lanes, z * lanes + part)
        value = params[row_up : row_up + 1, at]
        for s in range(1, quads):
            value = jnp.where(member == s, params[row_up + s : row_up + s + 1, at], value)
        bias[:, z * part : (z + 1) * part] = jnp.broadcast_to(value, (8, part))
    fill(padded, features, outer, inner, width)

    def chunk(i, carry):
        at = pl.ds(pl.multiple_of(i * lanes, lanes), lanes)
        sums = slide(padded, params, height, width, at, False)
        for out in range(height):
            conv[out * width : (out + 1) * width, at] = (
                sums[out] + params[row_bias : row_bias + 1, at]
            )
        return carry

    lax.fori_loop(0, chans // lanes, chunk, 0)

    def norm(i, carry):
        at = pl.ds(pl.multiple_of(i * width, width), width)
        value = conv[at, :]
        centered = value - jnp.mean(value, axis=1, keepdims=True)
        var = jnp.mean(centered * centered, axis=1, keepdims=True)
        scale = lax.rsqrt(var + eps)
        value = centered * scale
        normed[at, :] = value
        inv[at, :] = jnp.broadcast_to(scale, (width, lanes))
        normal[at, :] = (
            value * params[row_gain : row_gain + 1, 0:chans]
            + params[row_shift : row_shift + 1, 0:chans]
        ).astype(bf16)
        return carry

    lax.fori_loop(0, height, norm, 0)


def back_kernel(dconv, outer, inner, cotangent, params, out, padded):
    height, width, chans = dconv.shape
    fill(padded, dconv, outer, inner, width)

    def chunk(i, carry):
        at = pl.ds(pl.multiple_of(i * lanes, lanes), lanes)
        sums = slide(padded, params, height, width, at, True)
        for row in range(height):
            out[row, :, at] = (cotangent[row, :, at].astype(f32) + sums[row]).astype(bf16)
        return carry

    lax.fori_loop(0, chans // lanes, chunk, 0)


def taps_kernel(
    quads, layers, scale, dconv, features, outer, inner, cotangent, norms, upb, *refs
):
    out, padded, grads = refs
    height, width, chans = dconv.shape
    layer, member = place(quads)
    fill(padded, features, outer, inner, width)
    grads[...] = jnp.zeros_like(grads)

    def fold(value):
        return jnp.sum(value.reshape(width // 8, 8, lanes), axis=0)

    def chunk(i, carry):
        at = pl.ds(pl.multiple_of(i * lanes, lanes), lanes)
        own = [dconv[row, :, at].astype(f32) for row in range(height)]
        for second in range(7):
            sums = [jnp.zeros((8, lanes), f32) for _ in range(7)]
            for row in range(height + 6):
                piece = padded[row, 5 + second : 5 + second + width, at]
                for out in range(height):
                    first = row - out
                    if 0 <= first < 7:
                        sums[first] = sums[first] + fold(own[out] * piece)
            for first in range(7):
                tap = first * 7 + second
                grads[tap : tap + 1, at] = (
                    jnp.sum(sums[first], axis=0, keepdims=True) * scale
                )
        total = fold(own[0])
        for row in range(1, height):
            total = total + fold(own[row])
        grads[row_bias : row_bias + 1, at] = jnp.sum(total, axis=0, keepdims=True) * scale
        total = fold(cotangent[0, :, at].astype(f32))
        for row in range(1, height):
            total = total + fold(cotangent[row, :, at].astype(f32))
        grads[row_down : row_down + 1, at] = jnp.sum(total, axis=0, keepdims=True) * scale
        grads[row_gain : row_gain + 1, at] = norms[0:1, at] * scale
        grads[row_shift : row_shift + 1, at] = norms[1:2, at] * scale
        return carry

    lax.fori_loop(0, chans // lanes, chunk, 0)
    part = upb.shape[1] // layers
    for z in range(layers):
        bias = upb[0:1, z * part : (z + 1) * part] * scale
        for s in range(quads):
            grads[row_up + s : row_up + s + 1, z * lanes : z * lanes + part] = jnp.where(
                member == s, bias, 0.0
            )
    for other in range(layers):
        at = pl.multiple_of(jnp.bitwise_xor(layer, other) * lanes, lanes)
        out[other] = grads[:, pl.ds(at, lanes)]


def mlp_kernel(quads, layers, bias_row, *refs):
    normals, refs = refs[:quads], refs[quads:]
    cots, refs = refs[:quads], refs[quads:]
    weights, (total, even, odd, act, upb, down, up) = refs[:-7], refs[-7:]
    layer, _ = place(quads)
    cells, chans = normals[0].shape
    hidden_units = act.shape[1]
    part = hidden_units // layers
    for step in range(layers):
        source = lax.rem(layer - step + layers, layers)
        if len(weights) == layers:
            one, two = weights[step].at[0:part], weights[step].at[part:]
        else:
            one, two = weights[step], weights[layers + step]
        down[pl.ds(pl.multiple_of(source * part, part), part), :] = one[...]
        up[pl.ds(pl.multiple_of(source * lanes, lanes), lanes), :] = two[...]
    bias = bias_row[0:1, :]
    bias_sum = jnp.zeros((1, hidden_units), f32)
    for i in range(quads):
        hidden = jnp.dot(normals[i][...], up[...], preferred_element_type=f32) + bias
        dact = lax.dot_general(
            cots[i][...], down[...], (((1,), (1,)), ((), ())), preferred_element_type=f32
        )
        cumulative = 0.5 * (1.0 + lax.erf(hidden * (1.0 / math.sqrt(2.0))))
        density = jnp.exp(-0.5 * hidden * hidden) * (1.0 / math.sqrt(2.0 * math.pi))
        act[i * cells : (i + 1) * cells, :] = (hidden * cumulative).astype(bf16)
        dhidden = (dact * (cumulative + hidden * density)).astype(bf16)
        bias_sum = bias_sum + jnp.sum(dhidden.astype(f32), axis=0, keepdims=True)
        dnorm = lax.dot_general(
            dhidden, up[...], (((1,), (1,)), ((), ())), preferred_element_type=f32
        )
        at = slice(i // 2 * cells, (i // 2 + 1) * cells)
        if i % 2:
            odd[at, :] = dnorm.astype(bf16)
        else:
            even[at, :] = dnorm
        grad = lax.dot_general(
            normals[i][...], dhidden, (((0,), (0,)), ((), ())), preferred_element_type=f32
        )
        total[...] = grad if i == 0 else total[...] + grad
    upb[...] = jnp.broadcast_to(bias_sum, upb.shape)


def out_kernel(quads, layers, scale, total_up, act, down, *refs):
    cots, refs = refs[:quads], refs[quads:]
    own_down, own_up, refs = refs[0], refs[1], refs[2:]
    sends, (even, odd, total) = refs[:-3], refs[-3:]
    layer, _ = place(quads)
    cells = cots[0].shape[0]
    part = down.shape[0] // layers
    for i in range(quads):
        block = act[i * cells : (i + 1) * cells, :]
        grad = lax.dot_general(
            block, cots[i][...], (((0,), (0,)), ((), ())), preferred_element_type=f32
        )
        total[...] = grad if i == 0 else total[...] + grad
    for step in range(layers):
        if step == 0:
            one, two = own_down, own_up
        elif len(sends) == layers - 1:
            one, two = sends[step - 1].at[0:part], sends[step - 1].at[part:]
        else:
            one, two = sends[step - 1], sends[layers - 2 + step]
        to = lax.rem(layer + step, layers)
        piece = total[pl.ds(pl.multiple_of(to * part, part), part), :] * scale
        one[...] = piece.astype(one.dtype)
        piece = total_up[pl.ds(pl.multiple_of(to * lanes, lanes), lanes), :] * scale
        two[...] = piece.astype(two.dtype)
    for i in range(quads):
        block = act[i * cells : (i + 1) * cells, :]
        mixed = jnp.dot(block, down[...], preferred_element_type=f32)
        at = slice(i // 2 * cells, (i // 2 + 1) * cells)
        if i % 2:
            odd[at, :] = mixed.astype(bf16)
        else:
            even[at, :] = mixed


def norm_back_kernel(normed, inv, params, *refs):
    parts, (dconv, norms) = refs[:-2], refs[-2:]
    height, width, chans = dconv.shape
    gain_sum = jnp.zeros((1, chans), f32)
    shift_sum = jnp.zeros((1, chans), f32)
    for row in range(height):
        at = slice(row * width, (row + 1) * width)
        dnorm = parts[0][at, :].astype(f32)
        for part in parts[1:]:
            dnorm = dnorm + part[at, :].astype(f32)
        value = normed[at, :]
        gain_sum = gain_sum + jnp.sum(dnorm * value, axis=0, keepdims=True)
        shift_sum = shift_sum + jnp.sum(dnorm, axis=0, keepdims=True)
        scaled = dnorm * params[row_gain : row_gain + 1, 0:chans]
        mean = jnp.mean(scaled, axis=1, keepdims=True)
        cross = jnp.mean(scaled * value, axis=1, keepdims=True)
        dconv[row, :, :] = (inv[at, 0:1] * (scaled - mean - value * cross)).astype(bf16)
    norms[0:1, :] = gain_sum
    norms[1:2, :] = shift_sum


def up_split_kernel(quads, part, *refs):
    own_down, own_up, refs = refs[0], refs[1], refs[2:]
    terms, out_down, outs = refs[: -quads - 1], refs[-quads - 1], refs[-quads:]
    _, member = place(quads)
    if terms[0].shape[0] > lanes:
        downs = [term.at[0:part] for term in terms]
        ups = [term.at[part:] for term in terms]
    else:
        downs, ups = terms[: len(terms) // 2], terms[len(terms) // 2 :]
    total = own_down[...]
    for term in downs:
        total = total + term[...].astype(f32)
    out_down[...] = total
    own = outs[0].shape[0]
    for other, out in enumerate(outs):
        row = pl.multiple_of(jnp.bitwise_xor(member, other) * own, own)
        piece = own_up[pl.ds(row, own), :]
        for term in ups:
            piece = piece + term[pl.ds(row, own), :].astype(f32)
        out[...] = piece.astype(out.dtype)


def up_join_kernel(quads, layers, *refs):
    pieces, out = refs[:-1], refs[-1]
    _, member = place(quads)
    part = out.shape[1] // (quads * layers)
    for s in range(quads):
        held = pieces[s][...].astype(f32)
        for m in range(1, quads):
            held = jnp.where(member == m, pieces[s ^ m][...].astype(f32), held)
        for z in range(layers):
            at = (z * quads + s) * part
            out[:, at : at + part] = held[:, z * part : (z + 1) * part]


def small_kernel(quads, part_up, *refs):
    parts, outs = refs[:-6], refs[-6:]
    _, member = place(quads)
    total = parts[0][...]
    for part in parts[1:]:
        total = total + part[...]
    own = outs[0].shape[0]
    down = lax.broadcasted_iota(jnp.int32, (lanes, own), 0)
    across = lax.broadcasted_iota(jnp.int32, (lanes, own), 1)
    pick = (down == across + member * own).astype(f32)
    mine = jnp.dot(total, pick, preferred_element_type=f32, precision=lax.Precision.HIGHEST)
    outs[0][...] = lax.dot_general(
        pick,
        total[0:taps, :],
        (((0,), (1,)), ((), ())),
        preferred_element_type=f32,
        precision=lax.Precision.HIGHEST,
    )
    for row, out in zip((row_bias, row_gain, row_shift, row_down), outs[1:5]):
        out[...] = mine[row : row + 1, :]
    at = lax.broadcasted_iota(jnp.int32, total.shape, 0)
    chosen = jnp.where(at == row_up + member, total, 0.0)
    outs[5][...] = jnp.sum(chosen, axis=0, keepdims=True)[:, 0:part_up]


def per_device(
    features,
    cotangent,
    depth_weight,
    depth_bias,
    norm_gain,
    norm_shift,
    up_weight,
    up_bias,
    down_weight,
    down_bias,
):
    height, width, chans = features.shape
    devices = lax.axis_size("row")
    own, hidden_units = up_weight.shape
    part = down_weight.shape[0]
    layers = chans // lanes
    quads = devices // layers
    share = layers * part
    cells = height * width
    scale = 1.0 / math.sqrt(cells * devices)
    rows = round_up(row_up + quads, 16)

    def swap(value, other):
        return lax.ppermute(value, "row", [(i, i ^ other) for i in range(devices)])

    def turn(value, step=1):
        pairs = [
            (i, (i // quads + step) % layers * quads + i % quads) for i in range(devices)
        ]
        return lax.ppermute(value, "row", pairs)

    def halo(value):
        pairs = [(i, i + 1) for i in range(1, devices - 1, 2)]
        pairs = pairs + [(target, source) for source, target in pairs]
        return lax.ppermute(value, "row", pairs), swap(value, 1)

    def cross(value, other):
        return lax.ppermute(
            value, "row", [(i, (i // quads ^ other) * quads + i % quads) for i in range(devices)]
        )

    def add(one, two, kind):
        return (one.astype(f32) + two.astype(f32)).astype(kind)

    bits = []
    while 1 << len(bits) < quads:
        bits.append(1 << len(bits))

    def exchange(pieces, bit, extra=None):
        keys = sorted(key for key in pieces if key[0] & bit)
        blocks = [pieces[key] for key in keys]
        ahead, size = 0, blocks[0].shape[0]
        if extra is not None and extra.shape[1] == blocks[0].shape[1]:
            ahead = extra.shape[0]
            got = swap(jnp.concatenate([extra] + blocks, axis=0), bit)
            extra = got[:ahead]
        else:
            got = swap(jnp.concatenate(blocks, axis=0), bit)
            extra = None if extra is None else swap(extra, bit)
        kept = {key: piece for key, piece in pieces.items() if not key[0] & bit}
        for i, (target, source) in enumerate(keys):
            at = ahead + i * size
            kept[target ^ bit, source ^ bit] = got[at : at + size]
        return kept, extra

    def spread(held, bits):
        for bit in reversed(bits):
            held.update({i ^ bit: swap(block, bit) for i, block in list(held.items())})

    def near(even, odd):
        return even, swap(odd, bits[0])

    def far(even, odd):
        held = add(even, odd, f32).reshape(-1, cells, chans)
        for bit in bits[1:-1]:
            pairs = held.reshape(-1, 2, cells, chans)
            held = pairs[:, 0] + swap(pairs[:, 1].astype(bf16), bit).astype(f32)
        return held[0], held[1].astype(bf16)

    step = round_up(own, 16)
    block = layers * step
    *pieces, small, far_pack = call(
        functools.partial(pack_kernel, quads, layers, rows),
        [((block, lanes), bf16)] * (quads // 2)
        + [((rows, lanes), bf16), ((rows + quads // 2 * block, lanes), bf16)],
        (
            depth_weight.T,
            depth_bias.reshape(1, own),
            norm_gain.reshape(1, own),
            norm_shift.reshape(1, own),
            down_bias.reshape(1, own),
            up_bias.reshape(1, part),
            up_weight,
        ),
        [pltpu.VMEM((rows, own), f32), pltpu.VMEM((rows, lanes), f32)]
        + [pltpu.VMEM((own, taps), bf16)]
        + [pltpu.VMEM((1, own), bf16)] * 4
        + [pltpu.VMEM((1, part), bf16), pltpu.VMEM((own, hidden_units), bf16)]
        + [pltpu.SemaphoreType.DMA((7,))],
        space=pl.ANY,
        mib=60,
    )
    features, cotangent, down_weight = lax.optimization_barrier(
        (features, cotangent, down_weight, small)
    )[:3]
    got = swap(far_pack, bits[-1])
    pieces = {(i, 0): piece for i, piece in enumerate(pieces)}
    for i in range(quads // 2):
        pieces[i, bits[-1]] = got[rows + i * block : rows + (i + 1) * block]
    small = small + got[:rows]
    small, pieces = lax.optimization_barrier((small, pieces))
    for bit in reversed(bits[:-1]):
        pieces, got = exchange(pieces, bit, small)
        small = small + got
    small, pieces = lax.optimization_barrier((small, pieces))
    merged = share == chans and own % 16 == 0 and part % own == 0
    (up,) = call(
        functools.partial(unpack_kernel, quads, layers),
        [(((part // own if merged else 0) + quads, own, share), bf16)],
        [down_weight] + [pieces[0, i] for i in range(quads)],
    )
    up = up.reshape(-1, share)
    weights = [[up]] if merged else [[down_weight], [up]]
    for held in weights:
        held.extend(turn(held[0], step) for step in range(1, layers))
    outer, inner = halo(features)
    cots = {0: cotangent.reshape(cells, chans)}
    spread(cots, bits[1:])
    smalls = small
    other = 1
    while other < layers:
        smalls = jnp.concatenate([smalls, cross(smalls, other)], axis=0)
        other *= 2
    first = [held[1] for held in weights]
    smalls, first = lax.optimization_barrier((smalls, first))
    for held, value in zip(weights, first):
        held[1] = value
    smalls = [smalls[i * rows : (i + 1) * rows] for i in range(layers)]

    rim = (height + 6, width + 16, chans)
    normal, normed, inv, params, bias = call(
        functools.partial(conv_kernel, quads, layers),
        [
            ((cells, chans), bf16),
            ((cells, chans), f32),
            ((cells, lanes), f32),
            ((rows, chans), f32),
            ((8, share), f32),
        ],
        (features, outer, inner, *smalls),
        [pltpu.VMEM(rim, f32), pltpu.VMEM((cells, chans), f32)],
    )
    first = [held[-1] for held in weights]
    normal, cots, first = lax.optimization_barrier((normal, cots, first))
    for held, value in zip(weights, first):
        held[-1] = value
    normals = {0: normal}
    spread(normals, bits[1:])
    normals, weights = lax.optimization_barrier((normals, weights))
    spread(cots, bits[:1])
    spread(normals, bits[:1])
    normals, cots = ([held[i] for i in range(quads)] for held in (normals, cots))

    half = quads // 2 * cells
    total_up, even, odd, act, upb, down_full = call(
        functools.partial(mlp_kernel, quads, layers),
        [((chans, share), f32), ((half, chans), f32), ((half, chans), bf16)]
        + [((quads * cells, share), bf16), ((8, share), f32), ((share, chans), bf16)],
        (bias, *normals, *cots, *(block for held in weights for block in held)),
        [pltpu.VMEM((chans, share), bf16)],
        mib=40,
    )
    sums = near(even, odd)
    if merged:
        shapes = [(part + lanes, chans)] * (layers - 1)
    else:
        shapes = [(part, chans)] * (layers - 1) + [(lanes, share)] * (layers - 1)
    own_down, own_up, *sends, even, odd = call(
        functools.partial(out_kernel, quads, layers, scale),
        [((part, chans), f32), ((lanes, share), f32)]
        + [(shape, bf16) for shape in shapes]
        + [((half, chans), f32), ((half, chans), bf16)],
        (total_up, act, down_full, *cots),
        [pltpu.VMEM((share, chans), f32)],
        mib=40,
    )
    sums, sends = lax.optimization_barrier((sums, sends))
    kept, sent = far(*sums)
    dnorms = [kept, swap(sent, bits[-1])]
    terms = [turn(send, i % (layers - 1) + 1) for i, send in enumerate(sends)]
    mixed, across = far(*near(even, odd))
    across = swap(across, bits[-1])
    dnorms, terms[0] = lax.optimization_barrier((dnorms, terms[0]))

    dconv, norms = call(
        norm_back_kernel,
        [((height, width, chans), bf16), ((8, chans), f32)],
        (normed, inv, params, *dnorms),
    )
    (total,) = call(
        functools.partial(taps_kernel, quads, layers, scale),
        [((layers, rows, lanes), f32)],
        (dconv, features, outer, inner, cotangent, norms, upb),
        [pltpu.VMEM(rim, f32), pltpu.VMEM((rows, chans), f32)],
    )
    total, dconv, across, terms[2:] = lax.optimization_barrier(
        (total, dconv, across, terms[2:])
    )
    outer_back, inner_back = halo(dconv)
    for bit in bits:
        total = total + swap(total, bit)
    total, terms, inner_back = lax.optimization_barrier((total, terms, inner_back))
    grad_down_weight, *pieces = call(
        functools.partial(up_split_kernel, quads, part),
        [((part, chans), f32), ((own, share), f32)] + [((own, share), bf16)] * (quads - 1),
        (own_down, own_up, *terms),
    )
    pieces = {(i, 0): piece for i, piece in enumerate(pieces)}
    pieces, _ = exchange(pieces, bits[-1])
    while total.shape[0] > 2:
        middle = total.shape[0] // 2
        total = total[:middle] + cross(total[middle:], middle)
    (grad_features,) = call(
        back_kernel,
        [((height, width, chans), bf16)],
        (dconv, outer_back, inner_back, cotangent, params),
        [pltpu.VMEM(rim, f32)],
    )
    block_out = (
        features.astype(f32)
        + (mixed + across.astype(f32) + params[row_down, 0:chans]).reshape(height, width, chans)
    ).astype(bf16)
    total, grad_features, block_out, pieces = lax.optimization_barrier(
        (total, grad_features, block_out, pieces)
    )
    last = cross(total[1], 1)
    total = total[0]
    for bit in reversed(bits[:-1]):
        pieces, _ = exchange(pieces, bit)
    small_outs = call(
        functools.partial(small_kernel, quads, part),
        [((own, taps), f32)] + [((1, own), f32)] * 4 + [((1, part), f32)],
        (total, last),
    )
    grad_depth_weight = small_outs[0].T
    grad_depth_bias, grad_norm_gain, grad_norm_shift, grad_down_bias, grad_up_bias = (
        value.reshape(-1) for value in small_outs[1:]
    )

    (grad_up_weight,) = call(
        functools.partial(up_join_kernel, quads, layers),
        [((own, hidden_units), f32)],
        [pieces[0, i] for i in range(quads)],
    )
    return (
        block_out,
        grad_features,
        grad_up_weight,
        grad_down_weight,
        grad_depth_weight,
        grad_depth_bias,
        grad_norm_gain,
        grad_norm_shift,
        grad_up_bias,
        grad_down_bias,
    )


def solution(mesh):
    placed = (
        P(("groups", "row"), None, None),
        P(("groups", "row"), None, None),
        P(None, "row"),
        P("row"),
        P("row"),
        P("row"),
        P("row", None),
        P("row"),
        P("row", None),
        P("row"),
    )
    return jax.shard_map(
        per_device,
        mesh=mesh,
        in_specs=placed,
        out_specs=(
            P(("groups", "row"), None, None),
            P(("groups", "row"), None, None),
            P(("groups", "row"), None),
            P(("groups", "row"), None),
            P("groups", "row"),
            P(("groups", "row")),
            P(("groups", "row")),
            P(("groups", "row")),
            P(("groups", "row")),
            P(("groups", "row")),
        ),
        check_vma=False,
    )
```

```python
import functools
import math

import jax
import jax.numpy as jnp
from jax import lax
from jax.experimental import pallas as pl
from jax.experimental.pallas import tpu as pltpu
from jax.sharding import PartitionSpec as P

eps = 1e-06
lanes = 128
taps = 49
f32 = jnp.float32
bf16 = jnp.bfloat16
row_bias, row_gain, row_shift, row_down, row_up = 49, 50, 51, 52, 53


def round_up(value, unit):
    return (value + unit - 1) // unit * unit


def call(kernel, outs, args, scratch=(), mib=24, flops=1000, moved=1000, space=pltpu.VMEM):
    return pl.pallas_call(
        kernel,
        out_shape=[jax.ShapeDtypeStruct(shape, dtype) for shape, dtype in outs],
        in_specs=[pl.BlockSpec(memory_space=space)] * len(args),
        out_specs=[pl.BlockSpec(memory_space=pltpu.VMEM)] * len(outs),
        scratch_shapes=list(scratch),
        compiler_params=pltpu.CompilerParams(vmem_limit_bytes=mib * 1024 * 1024),
        cost_estimate=pl.CostEstimate(flops=flops, bytes_accessed=moved, transcendentals=0),
    )(*args)


def place(quads):
    index = lax.axis_index("row")
    return index // quads, lax.rem(index, quads)


def one_hot(rows, columns, offset):
    down = lax.broadcasted_iota(jnp.int32, (rows, columns), 0)
    across = lax.broadcasted_iota(jnp.int32, (rows, columns), 1)
    return (across == down + offset).astype(f32)


def pack_kernel(quads, layers, rows, *refs):
    given, refs = refs[:7], refs[7:]
    near, small, far, (held, head, *local), sems = (
        refs[: quads // 2],
        refs[quads // 2],
        refs[quads // 2 + 1],
        refs[quads // 2 + 2 : -1],
        refs[-1],
    )
    copies = [
        pltpu.make_async_copy(source, target, sems.at[i])
        for i, (source, target) in enumerate(zip(given, local))
    ]
    for copy in copies:
        copy.start()
    for copy in copies:
        copy.wait()
    dw, db, gain, shift, down, upb, up = local
    _, member = place(quads)
    own = dw.shape[0]
    part = upb.shape[1]
    step = round_up(own, 16)
    spread = one_hot(own, lanes, member * own).astype(bf16)
    held[...] = jnp.zeros_like(held)
    held[row_bias : row_bias + 1, :] = db[...].astype(f32)
    held[row_gain : row_gain + 1, :] = gain[...].astype(f32)
    held[row_shift : row_shift + 1, :] = shift[...].astype(f32)
    held[row_down : row_down + 1, :] = down[...].astype(f32)
    head[...] = jnp.dot(held[...].astype(bf16), spread, preferred_element_type=f32)
    head[0:taps, :] = lax.dot_general(
        dw[...], spread, (((0,), (0,)), ((), ())), preferred_element_type=f32
    )
    for s in range(quads):
        head[row_up + s : row_up + s + 1, 0:part] = jnp.where(
            member == s, upb[...].astype(f32), 0.0
        )
    small[...] = head[...].astype(bf16)
    far[0:rows, :] = head[...].astype(bf16)
    wide = [up[:, i * part : (i + 1) * part] for i in range(layers * quads)]
    for other in range(quads):
        partner = jnp.bitwise_xor(member, other)
        if other < quads // 2:
            out, base = near[other], 0
        else:
            out, base = far, rows + (other - quads // 2) * layers * step
        if step != own or part != lanes:
            out[base : base + layers * step, :] = jnp.zeros((layers * step, lanes), bf16)
        for z in range(layers):
            piece = wide[z * quads]
            for s in range(1, quads):
                piece = jnp.where(partner == s, wide[z * quads + s], piece)
            out[base + z * step : base + z * step + own, 0:part] = piece


def unpack_kernel(quads, layers, down, *refs):
    pieces, out = refs[:-1], refs[-1]
    _, member = place(quads)
    blocks, own, share = out.shape
    ahead = blocks - quads
    part = share // layers
    step = round_up(own, 16)
    for i in range(ahead):
        out[i] = down[i * own : (i + 1) * own, :]
    for other, piece in enumerate(pieces):
        to = ahead + jnp.bitwise_xor(member, other)
        for z in range(layers):
            block = piece[z * step : (z + 1) * step, :]
            out[to, :, z * part : (z + 1) * part] = block[0:own, 0:part]


def fill(padded, block, outer, inner, width):
    height = block.shape[0]
    even = lax.rem(lax.axis_index("row"), 2) == 0
    rows, columns, chans = padded.shape
    zero = jnp.zeros((rows, 8, chans), f32)
    padded[:, 0:8, :] = zero
    padded[:, 8 + width :, :] = jnp.zeros((rows, columns - 8 - width, chans), f32)
    low = jnp.where(even, outer[height - 3 :, :, :], inner[height - 3 :, :, :])
    high = jnp.where(even, inner[0:3, :, :], outer[0:3, :, :])
    padded[0:3, 8 : 8 + width, :] = low.astype(f32)
    padded[3 : 3 + height, 8 : 8 + width, :] = block[...].astype(f32)
    padded[3 + height :, 8 : 8 + width, :] = high.astype(f32)


def slide(padded, weights, height, width, at, flip):
    tiles = (width // 8, 8, lanes)
    sums = [jnp.zeros(tiles, f32) for _ in range(height)]
    for second in range(7):
        order = [first * 7 + second for first in range(7)]
        order = [taps - 1 - tap if flip else tap for tap in order]
        held = [jnp.broadcast_to(weights[tap : tap + 1, at], tiles[1:]) for tap in order]
        for row in range(height + 6):
            piece = padded[row, 5 + second : 5 + second + width, at].reshape(tiles)
            for out in range(height):
                if 0 <= row - out < 7:
                    sums[out] = sums[out] + piece * held[row - out]
    return [value.reshape(width, lanes) for value in sums]


def conv_kernel(quads, layers, features, outer, inner, *refs):
    smalls, (normal, normed, inv, params, bias, padded, conv) = refs[:-7], refs[-7:]
    height, width, chans = features.shape
    layer, member = place(quads)
    for other, small in enumerate(smalls):
        at = pl.multiple_of(jnp.bitwise_xor(layer, other) * lanes, lanes)
        params[:, pl.ds(at, lanes)] = small[...].astype(f32)
    part = bias.shape[1] // layers
    for z in range(layers):
        at = slice(z * lanes, z * lanes + part)
        value = params[row_up : row_up + 1, at]
        for s in range(1, quads):
            value = jnp.where(member == s, params[row_up + s : row_up + s + 1, at], value)
        bias[:, z * part : (z + 1) * part] = jnp.broadcast_to(value, (8, part))
    fill(padded, features, outer, inner, width)

    def chunk(i, carry):
        at = pl.ds(pl.multiple_of(i * lanes, lanes), lanes)
        sums = slide(padded, params, height, width, at, False)
        for out in range(height):
            conv[out * width : (out + 1) * width, at] = (
                sums[out] + params[row_bias : row_bias + 1, at]
            )
        return carry

    lax.fori_loop(0, chans // lanes, chunk, 0)

    def norm(i, carry):
        at = pl.ds(pl.multiple_of(i * width, width), width)
        value = conv[at, :]
        centered = value - jnp.mean(value, axis=1, keepdims=True)
        var = jnp.mean(centered * centered, axis=1, keepdims=True)
        scale = lax.rsqrt(var + eps)
        value = centered * scale
        normed[at, :] = value
        inv[at, :] = jnp.broadcast_to(scale, (width, lanes))
        normal[at, :] = (
            value * params[row_gain : row_gain + 1, 0:chans]
            + params[row_shift : row_shift + 1, 0:chans]
        ).astype(bf16)
        return carry

    lax.fori_loop(0, height, norm, 0)


def back_kernel(dconv, outer, inner, cotangent, params, out, padded):
    height, width, chans = dconv.shape
    fill(padded, dconv, outer, inner, width)

    def chunk(i, carry):
        at = pl.ds(pl.multiple_of(i * lanes, lanes), lanes)
        sums = slide(padded, params, height, width, at, True)
        for row in range(height):
            out[row, :, at] = (cotangent[row, :, at].astype(f32) + sums[row]).astype(bf16)
        return carry

    lax.fori_loop(0, chans // lanes, chunk, 0)


def taps_kernel(
    quads, layers, scale, dconv, features, outer, inner, cotangent, norms, upb, *refs
):
    out, padded, grads = refs
    height, width, chans = dconv.shape
    layer, member = place(quads)
    fill(padded, features, outer, inner, width)
    grads[...] = jnp.zeros_like(grads)

    def fold(value):
        return jnp.sum(value.reshape(width // 8, 8, lanes), axis=0)

    def chunk(i, carry):
        at = pl.ds(pl.multiple_of(i * lanes, lanes), lanes)
        own = [dconv[row, :, at].astype(f32) for row in range(height)]
        for second in range(7):
            sums = [jnp.zeros((8, lanes), f32) for _ in range(7)]
            for row in range(height + 6):
                piece = padded[row, 5 + second : 5 + second + width, at]
                for out in range(height):
                    first = row - out
                    if 0 <= first < 7:
                        sums[first] = sums[first] + fold(own[out] * piece)
            for first in range(7):
                tap = first * 7 + second
                grads[tap : tap + 1, at] = (
                    jnp.sum(sums[first], axis=0, keepdims=True) * scale
                )
        total = fold(own[0])
        for row in range(1, height):
            total = total + fold(own[row])
        grads[row_bias : row_bias + 1, at] = jnp.sum(total, axis=0, keepdims=True) * scale
        total = fold(cotangent[0, :, at].astype(f32))
        for row in range(1, height):
            total = total + fold(cotangent[row, :, at].astype(f32))
        grads[row_down : row_down + 1, at] = jnp.sum(total, axis=0, keepdims=True) * scale
        grads[row_gain : row_gain + 1, at] = norms[0:1, at] * scale
        grads[row_shift : row_shift + 1, at] = norms[1:2, at] * scale
        return carry

    lax.fori_loop(0, chans // lanes, chunk, 0)
    part = upb.shape[1] // layers
    for z in range(layers):
        bias = upb[0:1, z * part : (z + 1) * part] * scale
        for s in range(quads):
            grads[row_up + s : row_up + s + 1, z * lanes : z * lanes + part] = jnp.where(
                member == s, bias, 0.0
            )
    for other in range(layers):
        at = pl.multiple_of(jnp.bitwise_xor(layer, other) * lanes, lanes)
        out[other] = grads[:, pl.ds(at, lanes)]


def mlp_kernel(quads, layers, bias_row, *refs):
    normals, refs = refs[:quads], refs[quads:]
    cots, refs = refs[:quads], refs[quads:]
    weights, (total, even, odd, act, upb, down, up) = refs[:-7], refs[-7:]
    layer, _ = place(quads)
    cells, chans = normals[0].shape
    hidden_units = act.shape[1]
    part = hidden_units // layers
    for step in range(layers):
        source = lax.rem(layer - step + layers, layers)
        if len(weights) == layers:
            one, two = weights[step].at[0:part], weights[step].at[part:]
        else:
            one, two = weights[step], weights[layers + step]
        down[pl.ds(pl.multiple_of(source * part, part), part), :] = one[...]
        up[pl.ds(pl.multiple_of(source * lanes, lanes), lanes), :] = two[...]
    bias = bias_row[0:1, :]
    bias_sum = jnp.zeros((1, hidden_units), f32)
    for i in range(quads):
        hidden = jnp.dot(normals[i][...], up[...], preferred_element_type=f32) + bias
        dact = lax.dot_general(
            cots[i][...], down[...], (((1,), (1,)), ((), ())), preferred_element_type=f32
        )
        cumulative = 0.5 * (1.0 + lax.erf(hidden * (1.0 / math.sqrt(2.0))))
        density = jnp.exp(-0.5 * hidden * hidden) * (1.0 / math.sqrt(2.0 * math.pi))
        act[i * cells : (i + 1) * cells, :] = (hidden * cumulative).astype(bf16)
        dhidden = (dact * (cumulative + hidden * density)).astype(bf16)
        bias_sum = bias_sum + jnp.sum(dhidden.astype(f32), axis=0, keepdims=True)
        dnorm = lax.dot_general(
            dhidden, up[...], (((1,), (1,)), ((), ())), preferred_element_type=f32
        )
        at = slice(i // 2 * cells, (i // 2 + 1) * cells)
        if i % 2:
            odd[at, :] = dnorm.astype(bf16)
        else:
            even[at, :] = dnorm
        grad = lax.dot_general(
            normals[i][...], dhidden, (((0,), (0,)), ((), ())), preferred_element_type=f32
        )
        total[...] = grad if i == 0 else total[...] + grad
    upb[...] = jnp.broadcast_to(bias_sum, upb.shape)


def out_kernel(quads, layers, scale, total_up, act, down, *refs):
    cots, refs = refs[:quads], refs[quads:]
    own_down, own_up, refs = refs[0], refs[1], refs[2:]
    sends, (even, odd, total) = refs[:-3], refs[-3:]
    layer, _ = place(quads)
    cells = cots[0].shape[0]
    part = down.shape[0] // layers
    for i in range(quads):
        block = act[i * cells : (i + 1) * cells, :]
        grad = lax.dot_general(
            block, cots[i][...], (((0,), (0,)), ((), ())), preferred_element_type=f32
        )
        total[...] = grad if i == 0 else total[...] + grad
    for step in range(layers):
        if step == 0:
            one, two = own_down, own_up
        elif len(sends) == layers - 1:
            one, two = sends[step - 1].at[0:part], sends[step - 1].at[part:]
        else:
            one, two = sends[step - 1], sends[layers - 2 + step]
        to = lax.rem(layer + step, layers)
        piece = total[pl.ds(pl.multiple_of(to * part, part), part), :] * scale
        one[...] = piece.astype(one.dtype)
        piece = total_up[pl.ds(pl.multiple_of(to * lanes, lanes), lanes), :] * scale
        two[...] = piece.astype(two.dtype)
    for i in range(quads):
        block = act[i * cells : (i + 1) * cells, :]
        mixed = jnp.dot(block, down[...], preferred_element_type=f32)
        at = slice(i // 2 * cells, (i // 2 + 1) * cells)
        if i % 2:
            odd[at, :] = mixed.astype(bf16)
        else:
            even[at, :] = mixed


def norm_back_kernel(normed, inv, params, *refs):
    parts, (dconv, norms) = refs[:-2], refs[-2:]
    height, width, chans = dconv.shape
    gain_sum = jnp.zeros((1, chans), f32)
    shift_sum = jnp.zeros((1, chans), f32)
    for row in range(height):
        at = slice(row * width, (row + 1) * width)
        dnorm = parts[0][at, :].astype(f32)
        for part in parts[1:]:
            dnorm = dnorm + part[at, :].astype(f32)
        value = normed[at, :]
        gain_sum = gain_sum + jnp.sum(dnorm * value, axis=0, keepdims=True)
        shift_sum = shift_sum + jnp.sum(dnorm, axis=0, keepdims=True)
        scaled = dnorm * params[row_gain : row_gain + 1, 0:chans]
        mean = jnp.mean(scaled, axis=1, keepdims=True)
        cross = jnp.mean(scaled * value, axis=1, keepdims=True)
        dconv[row, :, :] = (inv[at, 0:1] * (scaled - mean - value * cross)).astype(bf16)
    norms[0:1, :] = gain_sum
    norms[1:2, :] = shift_sum


def up_split_kernel(quads, part, *refs):
    own_down, own_up, refs = refs[0], refs[1], refs[2:]
    terms, out_down, outs = refs[: -quads - 1], refs[-quads - 1], refs[-quads:]
    _, member = place(quads)
    if terms[0].shape[0] > lanes:
        downs = [term.at[0:part] for term in terms]
        ups = [term.at[part:] for term in terms]
    else:
        downs, ups = terms[: len(terms) // 2], terms[len(terms) // 2 :]
    total = own_down[...]
    for term in downs:
        total = total + term[...].astype(f32)
    out_down[...] = total
    own = outs[0].shape[0]
    for other, out in enumerate(outs):
        row = pl.multiple_of(jnp.bitwise_xor(member, other) * own, own)
        piece = own_up[pl.ds(row, own), :]
        for term in ups:
            piece = piece + term[pl.ds(row, own), :].astype(f32)
        out[...] = piece.astype(out.dtype)


def up_join_kernel(quads, layers, *refs):
    pieces, out = refs[:-1], refs[-1]
    _, member = place(quads)
    part = out.shape[1] // (quads * layers)
    for s in range(quads):
        held = pieces[s][...].astype(f32)
        for m in range(1, quads):
            held = jnp.where(member == m, pieces[s ^ m][...].astype(f32), held)
        for z in range(layers):
            at = (z * quads + s) * part
            out[:, at : at + part] = held[:, z * part : (z + 1) * part]


def small_kernel(quads, part_up, *refs):
    parts, outs = refs[:-6], refs[-6:]
    _, member = place(quads)
    total = parts[0][...]
    for part in parts[1:]:
        total = total + part[...]
    own = outs[0].shape[0]
    down = lax.broadcasted_iota(jnp.int32, (lanes, own), 0)
    across = lax.broadcasted_iota(jnp.int32, (lanes, own), 1)
    pick = (down == across + member * own).astype(f32)
    mine = jnp.dot(total, pick, preferred_element_type=f32, precision=lax.Precision.HIGHEST)
    outs[0][...] = lax.dot_general(
        pick,
        total[0:taps, :],
        (((0,), (1,)), ((), ())),
        preferred_element_type=f32,
        precision=lax.Precision.HIGHEST,
    )
    for row, out in zip((row_bias, row_gain, row_shift, row_down), outs[1:5]):
        out[...] = mine[row : row + 1, :]
    at = lax.broadcasted_iota(jnp.int32, total.shape, 0)
    chosen = jnp.where(at == row_up + member, total, 0.0)
    outs[5][...] = jnp.sum(chosen, axis=0, keepdims=True)[:, 0:part_up]


def per_device(
    features,
    cotangent,
    depth_weight,
    depth_bias,
    norm_gain,
    norm_shift,
    up_weight,
    up_bias,
    down_weight,
    down_bias,
):
    height, width, chans = features.shape
    devices = lax.axis_size("row")
    own, hidden_units = up_weight.shape
    part = down_weight.shape[0]
    layers = chans // lanes
    quads = devices // layers
    share = layers * part
    cells = height * width
    scale = 1.0 / math.sqrt(cells * devices)
    rows = round_up(row_up + quads, 16)

    def swap(value, other):
        return lax.ppermute(value, "row", [(i, i ^ other) for i in range(devices)])

    def turn(value, step=1):
        pairs = [
            (i, (i // quads + step) % layers * quads + i % quads) for i in range(devices)
        ]
        return lax.ppermute(value, "row", pairs)

    def halo(value):
        pairs = [(i, i + 1) for i in range(1, devices - 1, 2)]
        pairs = pairs + [(target, source) for source, target in pairs]
        return lax.ppermute(value, "row", pairs), swap(value, 1)

    def cross(value, other):
        return lax.ppermute(
            value, "row", [(i, (i // quads ^ other) * quads + i % quads) for i in range(devices)]
        )

    def add(one, two, kind):
        return (one.astype(f32) + two.astype(f32)).astype(kind)

    bits = []
    while 1 << len(bits) < quads:
        bits.append(1 << len(bits))

    def exchange(pieces, bit, extra=None):
        keys = sorted(key for key in pieces if key[0] & bit)
        blocks = [pieces[key] for key in keys]
        ahead, size = 0, blocks[0].shape[0]
        if extra is not None and extra.shape[1] == blocks[0].shape[1]:
            ahead = extra.shape[0]
            got = swap(jnp.concatenate([extra] + blocks, axis=0), bit)
            extra = got[:ahead]
        else:
            got = swap(jnp.concatenate(blocks, axis=0), bit)
            extra = None if extra is None else swap(extra, bit)
        kept = {key: piece for key, piece in pieces.items() if not key[0] & bit}
        for i, (target, source) in enumerate(keys):
            at = ahead + i * size
            kept[target ^ bit, source ^ bit] = got[at : at + size]
        return kept, extra

    def spread(held, bits):
        for bit in reversed(bits):
            held.update({i ^ bit: swap(block, bit) for i, block in list(held.items())})

    def near(even, odd):
        return even, swap(odd, bits[0])

    def far(even, odd):
        held = add(even, odd, f32).reshape(-1, cells, chans)
        for bit in bits[1:-1]:
            pairs = held.reshape(-1, 2, cells, chans)
            held = pairs[:, 0] + swap(pairs[:, 1].astype(bf16), bit).astype(f32)
        return held[0], held[1].astype(bf16)

    step = round_up(own, 16)
    block = layers * step
    *pieces, small, far_pack = call(
        functools.partial(pack_kernel, quads, layers, rows),
        [((block, lanes), bf16)] * (quads // 2)
        + [((rows, lanes), bf16), ((rows + quads // 2 * block, lanes), bf16)],
        (
            depth_weight.T,
            depth_bias.reshape(1, own),
            norm_gain.reshape(1, own),
            norm_shift.reshape(1, own),
            down_bias.reshape(1, own),
            up_bias.reshape(1, part),
            up_weight,
        ),
        [pltpu.VMEM((rows, own), f32), pltpu.VMEM((rows, lanes), f32)]
        + [pltpu.VMEM((own, taps), bf16)]
        + [pltpu.VMEM((1, own), bf16)] * 4
        + [pltpu.VMEM((1, part), bf16), pltpu.VMEM((own, hidden_units), bf16)]
        + [pltpu.SemaphoreType.DMA((7,))],
        space=pl.ANY,
        mib=60,
    )
    features, cotangent, down_weight = lax.optimization_barrier(
        (features, cotangent, down_weight, small)
    )[:3]
    got = swap(far_pack, bits[-1])
    pieces = {(i, 0): piece for i, piece in enumerate(pieces)}
    for i in range(quads // 2):
        pieces[i, bits[-1]] = got[rows + i * block : rows + (i + 1) * block]
    small = small + got[:rows]
    small, pieces = lax.optimization_barrier((small, pieces))
    for bit in reversed(bits[:-1]):
        pieces, got = exchange(pieces, bit, small)
        small = small + got
    small, pieces = lax.optimization_barrier((small, pieces))
    merged = share == chans and own % 16 == 0 and part % own == 0
    (up,) = call(
        functools.partial(unpack_kernel, quads, layers),
        [(((part // own if merged else 0) + quads, own, share), bf16)],
        [down_weight] + [pieces[0, i] for i in range(quads)],
    )
    up = up.reshape(-1, share)
    weights = [[up]] if merged else [[down_weight], [up]]
    for held in weights:
        held.extend(turn(held[0], step) for step in range(1, layers))
    outer, inner = halo(features)
    cots = {0: cotangent.reshape(cells, chans)}
    spread(cots, bits[1:])
    smalls = small
    other = 1
    while other < layers:
        smalls = jnp.concatenate([smalls, cross(smalls, other)], axis=0)
        other *= 2
    first = [held[1] for held in weights]
    smalls, first = lax.optimization_barrier((smalls, first))
    for held, value in zip(weights, first):
        held[1] = value
    smalls = [smalls[i * rows : (i + 1) * rows] for i in range(layers)]

    rim = (height + 6, width + 16, chans)
    normal, normed, inv, params, bias = call(
        functools.partial(conv_kernel, quads, layers),
        [
            ((cells, chans), bf16),
            ((cells, chans), f32),
            ((cells, lanes), f32),
            ((rows, chans), f32),
            ((8, share), f32),
        ],
        (features, outer, inner, *smalls),
        [pltpu.VMEM(rim, f32), pltpu.VMEM((cells, chans), f32)],
    )
    normal, cots = lax.optimization_barrier((normal, cots))
    normals = {0: normal}
    spread(normals, bits[1:])
    normals, weights = lax.optimization_barrier((normals, weights))
    spread(cots, bits[:1])
    spread(normals, bits[:1])
    normals, cots = ([held[i] for i in range(quads)] for held in (normals, cots))

    half = quads // 2 * cells
    total_up, even, odd, act, upb, down_full = call(
        functools.partial(mlp_kernel, quads, layers),
        [((chans, share), f32), ((half, chans), f32), ((half, chans), bf16)]
        + [((quads * cells, share), bf16), ((8, share), f32), ((share, chans), bf16)],
        (bias, *normals, *cots, *(block for held in weights for block in held)),
        [pltpu.VMEM((chans, share), bf16)],
        mib=40,
    )
    sums = near(even, odd)
    if merged:
        shapes = [(part + lanes, chans)] * (layers - 1)
    else:
        shapes = [(part, chans)] * (layers - 1) + [(lanes, share)] * (layers - 1)
    own_down, own_up, *sends, even, odd = call(
        functools.partial(out_kernel, quads, layers, scale),
        [((part, chans), f32), ((lanes, share), f32)]
        + [(shape, bf16) for shape in shapes]
        + [((half, chans), f32), ((half, chans), bf16)],
        (total_up, act, down_full, *cots),
        [pltpu.VMEM((share, chans), f32)],
        mib=40,
    )
    sums, sends = lax.optimization_barrier((sums, sends))
    kept, sent = far(*sums)
    dnorms = [kept, swap(sent, bits[-1])]
    terms = [turn(send, i % (layers - 1) + 1) for i, send in enumerate(sends)]
    sums = near(even, odd)
    dnorms, sums = lax.optimization_barrier((dnorms, sums))
    mixed, across = far(*sums)
    across = swap(across, bits[-1])

    dconv, norms = call(
        norm_back_kernel,
        [((height, width, chans), bf16), ((8, chans), f32)],
        (normed, inv, params, *dnorms),
    )
    (total,) = call(
        functools.partial(taps_kernel, quads, layers, scale),
        [((layers, rows, lanes), f32)],
        (dconv, features, outer, inner, cotangent, norms, upb),
        [pltpu.VMEM(rim, f32), pltpu.VMEM((rows, chans), f32)],
    )
    for bit in bits[:-1]:
        total = total + swap(total, bit)
    total, dconv, across, terms[0], terms[2:] = lax.optimization_barrier(
        (total, dconv, across, terms[0], terms[2:])
    )
    outer_back, inner_back = halo(dconv)
    total = total + swap(total, bits[-1])
    total, terms, inner_back = lax.optimization_barrier((total, terms, inner_back))
    grad_down_weight, *pieces = call(
        functools.partial(up_split_kernel, quads, part),
        [((part, chans), f32), ((own, share), f32)] + [((own, share), bf16)] * (quads - 1),
        (own_down, own_up, *terms),
    )
    pieces = {(i, 0): piece for i, piece in enumerate(pieces)}
    pieces, _ = exchange(pieces, bits[-1])
    while total.shape[0] > 2:
        middle = total.shape[0] // 2
        total = total[:middle] + cross(total[middle:], middle)
    (grad_features,) = call(
        back_kernel,
        [((height, width, chans), bf16)],
        (dconv, outer_back, inner_back, cotangent, params),
        [pltpu.VMEM(rim, f32)],
    )
    block_out = (
        features.astype(f32)
        + (mixed + across.astype(f32) + params[row_down, 0:chans]).reshape(height, width, chans)
    ).astype(bf16)
    total, grad_features, block_out, pieces = lax.optimization_barrier(
        (total, grad_features, block_out, pieces)
    )
    last = cross(total[1], 1)
    for bit in reversed(bits[:-1]):
        pieces, _ = exchange(pieces, bit)
    (grad_up_weight,) = call(
        functools.partial(up_join_kernel, quads, layers),
        [((own, hidden_units), f32)],
        [pieces[0, i] for i in range(quads)],
    )
    total, grad_up_weight = lax.optimization_barrier((total[0], grad_up_weight))
    small_outs = call(
        functools.partial(small_kernel, quads, part),
        [((own, taps), f32)] + [((1, own), f32)] * 4 + [((1, part), f32)],
        (total, last),
    )
    grad_depth_weight = small_outs[0].T
    grad_depth_bias, grad_norm_gain, grad_norm_shift, grad_down_bias, grad_up_bias = (
        value.reshape(-1) for value in small_outs[1:]
    )

    return (
        block_out,
        grad_features,
        grad_up_weight,
        grad_down_weight,
        grad_depth_weight,
        grad_depth_bias,
        grad_norm_gain,
        grad_norm_shift,
        grad_up_bias,
        grad_down_bias,
    )


def solution(mesh):
    placed = (
        P(("groups", "row"), None, None),
        P(("groups", "row"), None, None),
        P(None, "row"),
        P("row"),
        P("row"),
        P("row"),
        P("row", None),
        P("row"),
        P("row", None),
        P("row"),
    )
    return jax.shard_map(
        per_device,
        mesh=mesh,
        in_specs=placed,
        out_specs=(
            P(("groups", "row"), None, None),
            P(("groups", "row"), None, None),
            P(("groups", "row"), None),
            P(("groups", "row"), None),
            P("groups", "row"),
            P(("groups", "row")),
            P(("groups", "row")),
            P(("groups", "row")),
            P(("groups", "row")),
            P(("groups", "row")),
        ),
        check_vma=False,
    )
```

```python
import functools
import math

import jax
import jax.numpy as jnp
from jax import lax
from jax.experimental import pallas as pl
from jax.experimental.pallas import tpu as pltpu
from jax.sharding import PartitionSpec as P

eps = 1e-06
lanes = 128
taps = 49
f32 = jnp.float32
bf16 = jnp.bfloat16
row_bias, row_gain, row_shift, row_down, row_up = 49, 50, 51, 52, 53


def round_up(value, unit):
    return (value + unit - 1) // unit * unit


def call(kernel, outs, args, scratch=(), mib=24, flops=1000, moved=1000, space=pltpu.VMEM):
    return pl.pallas_call(
        kernel,
        out_shape=[jax.ShapeDtypeStruct(shape, dtype) for shape, dtype in outs],
        in_specs=[pl.BlockSpec(memory_space=space)] * len(args),
        out_specs=[pl.BlockSpec(memory_space=pltpu.VMEM)] * len(outs),
        scratch_shapes=list(scratch),
        compiler_params=pltpu.CompilerParams(vmem_limit_bytes=mib * 1024 * 1024),
        cost_estimate=pl.CostEstimate(flops=flops, bytes_accessed=moved, transcendentals=0),
    )(*args)


def place(quads):
    index = lax.axis_index("row")
    return index // quads, lax.rem(index, quads)


def one_hot(rows, columns, offset):
    down = lax.broadcasted_iota(jnp.int32, (rows, columns), 0)
    across = lax.broadcasted_iota(jnp.int32, (rows, columns), 1)
    return (across == down + offset).astype(f32)


def pack_kernel(quads, layers, rows, *refs):
    given, refs = refs[:7], refs[7:]
    near, small, far, (held, head, *local), sems = (
        refs[: quads // 2],
        refs[quads // 2],
        refs[quads // 2 + 1],
        refs[quads // 2 + 2 : -1],
        refs[-1],
    )
    copies = [
        pltpu.make_async_copy(source, target, sems.at[i])
        for i, (source, target) in enumerate(zip(given, local))
    ]
    for copy in copies:
        copy.start()
    for copy in copies:
        copy.wait()
    dw, db, gain, shift, down, upb, up = local
    _, member = place(quads)
    own = dw.shape[0]
    part = upb.shape[1]
    step = round_up(own, 16)
    spread = one_hot(own, lanes, member * own).astype(bf16)
    held[...] = jnp.zeros_like(held)
    held[row_bias : row_bias + 1, :] = db[...].astype(f32)
    held[row_gain : row_gain + 1, :] = gain[...].astype(f32)
    held[row_shift : row_shift + 1, :] = shift[...].astype(f32)
    held[row_down : row_down + 1, :] = down[...].astype(f32)
    head[...] = jnp.dot(held[...].astype(bf16), spread, preferred_element_type=f32)
    head[0:taps, :] = lax.dot_general(
        dw[...], spread, (((0,), (0,)), ((), ())), preferred_element_type=f32
    )
    for s in range(quads):
        head[row_up + s : row_up + s + 1, 0:part] = jnp.where(
            member == s, upb[...].astype(f32), 0.0
        )
    small[...] = head[...].astype(bf16)
    far[0:rows, :] = head[...].astype(bf16)
    wide = [up[:, i * part : (i + 1) * part] for i in range(layers * quads)]
    for other in range(quads):
        partner = jnp.bitwise_xor(member, other)
        if other < quads // 2:
            out, base = near[other], 0
        else:
            out, base = far, rows + (other - quads // 2) * layers * step
        if step != own or part != lanes:
            out[base : base + layers * step, :] = jnp.zeros((layers * step, lanes), bf16)
        for z in range(layers):
            piece = wide[z * quads]
            for s in range(1, quads):
                piece = jnp.where(partner == s, wide[z * quads + s], piece)
            out[base + z * step : base + z * step + own, 0:part] = piece


def unpack_kernel(quads, layers, down, *refs):
    pieces, out = refs[:-1], refs[-1]
    _, member = place(quads)
    blocks, own, share = out.shape
    ahead = blocks - quads
    part = share // layers
    step = round_up(own, 16)
    for i in range(ahead):
        out[i] = down[i * own : (i + 1) * own, :]
    for other, piece in enumerate(pieces):
        to = ahead + jnp.bitwise_xor(member, other)
        for z in range(layers):
            block = piece[z * step : (z + 1) * step, :]
            out[to, :, z * part : (z + 1) * part] = block[0:own, 0:part]


def fill(padded, block, outer, inner, width):
    height = block.shape[0]
    even = lax.rem(lax.axis_index("row"), 2) == 0
    rows, columns, chans = padded.shape
    zero = jnp.zeros((rows, 8, chans), f32)
    padded[:, 0:8, :] = zero
    padded[:, 8 + width :, :] = jnp.zeros((rows, columns - 8 - width, chans), f32)
    low = jnp.where(even, outer[height - 3 :, :, :], inner[height - 3 :, :, :])
    high = jnp.where(even, inner[0:3, :, :], outer[0:3, :, :])
    padded[0:3, 8 : 8 + width, :] = low.astype(f32)
    padded[3 : 3 + height, 8 : 8 + width, :] = block[...].astype(f32)
    padded[3 + height :, 8 : 8 + width, :] = high.astype(f32)


def slide(padded, weights, height, width, at, flip):
    tiles = (width // 8, 8, lanes)
    sums = [jnp.zeros(tiles, f32) for _ in range(height)]
    for second in range(7):
        order = [first * 7 + second for first in range(7)]
        order = [taps - 1 - tap if flip else tap for tap in order]
        held = [jnp.broadcast_to(weights[tap : tap + 1, at], tiles[1:]) for tap in order]
        for row in range(height + 6):
            piece = padded[row, 5 + second : 5 + second + width, at].reshape(tiles)
            for out in range(height):
                if 0 <= row - out < 7:
                    sums[out] = sums[out] + piece * held[row - out]
    return [value.reshape(width, lanes) for value in sums]


def conv_kernel(quads, layers, features, outer, inner, *refs):
    smalls, (normal, normed, inv, params, bias, padded, conv) = refs[:-7], refs[-7:]
    height, width, chans = features.shape
    layer, member = place(quads)
    for other, small in enumerate(smalls):
        at = pl.multiple_of(jnp.bitwise_xor(layer, other) * lanes, lanes)
        params[:, pl.ds(at, lanes)] = small[...].astype(f32)
    part = bias.shape[1] // layers
    for z in range(layers):
        at = slice(z * lanes, z * lanes + part)
        value = params[row_up : row_up + 1, at]
        for s in range(1, quads):
            value = jnp.where(member == s, params[row_up + s : row_up + s + 1, at], value)
        bias[:, z * part : (z + 1) * part] = jnp.broadcast_to(value, (8, part))
    fill(padded, features, outer, inner, width)

    def chunk(i, carry):
        at = pl.ds(pl.multiple_of(i * lanes, lanes), lanes)
        sums = slide(padded, params, height, width, at, False)
        for out in range(height):
            conv[out * width : (out + 1) * width, at] = (
                sums[out] + params[row_bias : row_bias + 1, at]
            )
        return carry

    lax.fori_loop(0, chans // lanes, chunk, 0, unroll=True)

    def norm(i, carry):
        at = pl.ds(pl.multiple_of(i * width, width), width)
        value = conv[at, :]
        centered = value - jnp.mean(value, axis=1, keepdims=True)
        var = jnp.mean(centered * centered, axis=1, keepdims=True)
        scale = lax.rsqrt(var + eps)
        value = centered * scale
        normed[at, :] = value
        inv[at, :] = jnp.broadcast_to(scale, (width, lanes))
        normal[at, :] = (
            value * params[row_gain : row_gain + 1, 0:chans]
            + params[row_shift : row_shift + 1, 0:chans]
        ).astype(bf16)
        return carry

    lax.fori_loop(0, height, norm, 0, unroll=True)


def back_kernel(dconv, outer, inner, cotangent, params, out, padded):
    height, width, chans = dconv.shape
    fill(padded, dconv, outer, inner, width)

    def chunk(i, carry):
        at = pl.ds(pl.multiple_of(i * lanes, lanes), lanes)
        sums = slide(padded, params, height, width, at, True)
        for row in range(height):
            out[row, :, at] = (cotangent[row, :, at].astype(f32) + sums[row]).astype(bf16)
        return carry

    lax.fori_loop(0, chans // lanes, chunk, 0, unroll=True)


def taps_kernel(
    quads, layers, scale, dconv, features, outer, inner, cotangent, norms, upb, *refs
):
    out, padded, grads = refs
    height, width, chans = dconv.shape
    layer, member = place(quads)
    fill(padded, features, outer, inner, width)
    grads[...] = jnp.zeros_like(grads)

    def fold(value):
        return jnp.sum(value.reshape(width // 8, 8, lanes), axis=0)

    def chunk(i, carry):
        at = pl.ds(pl.multiple_of(i * lanes, lanes), lanes)
        own = [dconv[row, :, at].astype(f32) for row in range(height)]
        for second in range(7):
            sums = [jnp.zeros((8, lanes), f32) for _ in range(7)]
            for row in range(height + 6):
                piece = padded[row, 5 + second : 5 + second + width, at]
                for out in range(height):
                    first = row - out
                    if 0 <= first < 7:
                        sums[first] = sums[first] + fold(own[out] * piece)
            for first in range(7):
                tap = first * 7 + second
                grads[tap : tap + 1, at] = (
                    jnp.sum(sums[first], axis=0, keepdims=True) * scale
                )
        total = fold(own[0])
        for row in range(1, height):
            total = total + fold(own[row])
        grads[row_bias : row_bias + 1, at] = jnp.sum(total, axis=0, keepdims=True) * scale
        total = fold(cotangent[0, :, at].astype(f32))
        for row in range(1, height):
            total = total + fold(cotangent[row, :, at].astype(f32))
        grads[row_down : row_down + 1, at] = jnp.sum(total, axis=0, keepdims=True) * scale
        grads[row_gain : row_gain + 1, at] = norms[0:1, at] * scale
        grads[row_shift : row_shift + 1, at] = norms[1:2, at] * scale
        return carry

    lax.fori_loop(0, chans // lanes, chunk, 0, unroll=True)
    part = upb.shape[1] // layers
    for z in range(layers):
        bias = upb[0:1, z * part : (z + 1) * part] * scale
        for s in range(quads):
            grads[row_up + s : row_up + s + 1, z * lanes : z * lanes + part] = jnp.where(
                member == s, bias, 0.0
            )
    for other in range(layers):
        at = pl.multiple_of(jnp.bitwise_xor(layer, other) * lanes, lanes)
        out[other] = grads[:, pl.ds(at, lanes)]


def mlp_kernel(quads, layers, bias_row, *refs):
    normals, refs = refs[:quads], refs[quads:]
    cots, refs = refs[:quads], refs[quads:]
    weights, (total, even, odd, act, upb, down, up) = refs[:-7], refs[-7:]
    layer, _ = place(quads)
    cells, chans = normals[0].shape
    hidden_units = act.shape[1]
    part = hidden_units // layers
    for step in range(layers):
        source = lax.rem(layer - step + layers, layers)
        if len(weights) == layers:
            one, two = weights[step].at[0:part], weights[step].at[part:]
        else:
            one, two = weights[step], weights[layers + step]
        down[pl.ds(pl.multiple_of(source * part, part), part), :] = one[...]
        up[pl.ds(pl.multiple_of(source * lanes, lanes), lanes), :] = two[...]
    bias = bias_row[0:1, :]
    bias_sum = jnp.zeros((1, hidden_units), f32)
    for i in range(quads):
        hidden = jnp.dot(normals[i][...], up[...], preferred_element_type=f32) + bias
        dact = lax.dot_general(
            cots[i][...], down[...], (((1,), (1,)), ((), ())), preferred_element_type=f32
        )
        cumulative = 0.5 * (1.0 + lax.erf(hidden * (1.0 / math.sqrt(2.0))))
        density = jnp.exp(-0.5 * hidden * hidden) * (1.0 / math.sqrt(2.0 * math.pi))
        act[i * cells : (i + 1) * cells, :] = (hidden * cumulative).astype(bf16)
        dhidden = (dact * (cumulative + hidden * density)).astype(bf16)
        bias_sum = bias_sum + jnp.sum(dhidden.astype(f32), axis=0, keepdims=True)
        dnorm = lax.dot_general(
            dhidden, up[...], (((1,), (1,)), ((), ())), preferred_element_type=f32
        )
        at = slice(i // 2 * cells, (i // 2 + 1) * cells)
        if i % 2:
            odd[at, :] = dnorm.astype(bf16)
        else:
            even[at, :] = dnorm
        grad = lax.dot_general(
            normals[i][...], dhidden, (((0,), (0,)), ((), ())), preferred_element_type=f32
        )
        total[...] = grad if i == 0 else total[...] + grad
    upb[...] = jnp.broadcast_to(bias_sum, upb.shape)


def out_kernel(quads, layers, scale, total_up, act, down, *refs):
    cots, refs = refs[:quads], refs[quads:]
    own_down, own_up, refs = refs[0], refs[1], refs[2:]
    sends, (even, odd, total) = refs[:-3], refs[-3:]
    layer, _ = place(quads)
    cells = cots[0].shape[0]
    part = down.shape[0] // layers
    for i in range(quads):
        block = act[i * cells : (i + 1) * cells, :]
        grad = lax.dot_general(
            block, cots[i][...], (((0,), (0,)), ((), ())), preferred_element_type=f32
        )
        total[...] = grad if i == 0 else total[...] + grad
    for step in range(layers):
        if step == 0:
            one, two = own_down, own_up
        elif len(sends) == layers - 1:
            one, two = sends[step - 1].at[0:part], sends[step - 1].at[part:]
        else:
            one, two = sends[step - 1], sends[layers - 2 + step]
        to = lax.rem(layer + step, layers)
        piece = total[pl.ds(pl.multiple_of(to * part, part), part), :] * scale
        one[...] = piece.astype(one.dtype)
        piece = total_up[pl.ds(pl.multiple_of(to * lanes, lanes), lanes), :] * scale
        two[...] = piece.astype(two.dtype)
    for i in range(quads):
        block = act[i * cells : (i + 1) * cells, :]
        mixed = jnp.dot(block, down[...], preferred_element_type=f32)
        at = slice(i // 2 * cells, (i // 2 + 1) * cells)
        if i % 2:
            odd[at, :] = mixed.astype(bf16)
        else:
            even[at, :] = mixed


def norm_back_kernel(normed, inv, params, *refs):
    parts, (dconv, norms) = refs[:-2], refs[-2:]
    height, width, chans = dconv.shape
    gain_sum = jnp.zeros((1, chans), f32)
    shift_sum = jnp.zeros((1, chans), f32)
    for row in range(height):
        at = slice(row * width, (row + 1) * width)
        dnorm = parts[0][at, :].astype(f32)
        for part in parts[1:]:
            dnorm = dnorm + part[at, :].astype(f32)
        value = normed[at, :]
        gain_sum = gain_sum + jnp.sum(dnorm * value, axis=0, keepdims=True)
        shift_sum = shift_sum + jnp.sum(dnorm, axis=0, keepdims=True)
        scaled = dnorm * params[row_gain : row_gain + 1, 0:chans]
        mean = jnp.mean(scaled, axis=1, keepdims=True)
        cross = jnp.mean(scaled * value, axis=1, keepdims=True)
        dconv[row, :, :] = (inv[at, 0:1] * (scaled - mean - value * cross)).astype(bf16)
    norms[0:1, :] = gain_sum
    norms[1:2, :] = shift_sum


def up_split_kernel(quads, part, *refs):
    own_down, own_up, refs = refs[0], refs[1], refs[2:]
    terms, out_down, outs = refs[: -quads - 1], refs[-quads - 1], refs[-quads:]
    _, member = place(quads)
    if terms[0].shape[0] > lanes:
        downs = [term.at[0:part] for term in terms]
        ups = [term.at[part:] for term in terms]
    else:
        downs, ups = terms[: len(terms) // 2], terms[len(terms) // 2 :]
    total = own_down[...]
    for term in downs:
        total = total + term[...].astype(f32)
    out_down[...] = total
    own = outs[0].shape[0]
    for other, out in enumerate(outs):
        row = pl.multiple_of(jnp.bitwise_xor(member, other) * own, own)
        piece = own_up[pl.ds(row, own), :]
        for term in ups:
            piece = piece + term[pl.ds(row, own), :].astype(f32)
        out[...] = piece.astype(out.dtype)


def up_join_kernel(quads, layers, *refs):
    pieces, out = refs[:-1], refs[-1]
    _, member = place(quads)
    part = out.shape[1] // (quads * layers)
    for s in range(quads):
        held = pieces[s][...].astype(f32)
        for m in range(1, quads):
            held = jnp.where(member == m, pieces[s ^ m][...].astype(f32), held)
        for z in range(layers):
            at = (z * quads + s) * part
            out[:, at : at + part] = held[:, z * part : (z + 1) * part]


def small_kernel(quads, part_up, *refs):
    parts, outs = refs[:-6], refs[-6:]
    _, member = place(quads)
    total = parts[0][...]
    for part in parts[1:]:
        total = total + part[...]
    own = outs[0].shape[0]
    down = lax.broadcasted_iota(jnp.int32, (lanes, own), 0)
    across = lax.broadcasted_iota(jnp.int32, (lanes, own), 1)
    pick = (down == across + member * own).astype(f32)
    mine = jnp.dot(total, pick, preferred_element_type=f32, precision=lax.Precision.HIGHEST)
    outs[0][...] = lax.dot_general(
        pick,
        total[0:taps, :],
        (((0,), (1,)), ((), ())),
        preferred_element_type=f32,
        precision=lax.Precision.HIGHEST,
    )
    for row, out in zip((row_bias, row_gain, row_shift, row_down), outs[1:5]):
        out[...] = mine[row : row + 1, :]
    at = lax.broadcasted_iota(jnp.int32, total.shape, 0)
    chosen = jnp.where(at == row_up + member, total, 0.0)
    outs[5][...] = jnp.sum(chosen, axis=0, keepdims=True)[:, 0:part_up]


def per_device(
    features,
    cotangent,
    depth_weight,
    depth_bias,
    norm_gain,
    norm_shift,
    up_weight,
    up_bias,
    down_weight,
    down_bias,
):
    height, width, chans = features.shape
    devices = lax.axis_size("row")
    own, hidden_units = up_weight.shape
    part = down_weight.shape[0]
    layers = chans // lanes
    quads = devices // layers
    share = layers * part
    cells = height * width
    scale = 1.0 / math.sqrt(cells * devices)
    rows = round_up(row_up + quads, 16)

    def swap(value, other):
        return lax.ppermute(value, "row", [(i, i ^ other) for i in range(devices)])

    def turn(value, step=1):
        pairs = [
            (i, (i // quads + step) % layers * quads + i % quads) for i in range(devices)
        ]
        return lax.ppermute(value, "row", pairs)

    def halo(value):
        pairs = [(i, i + 1) for i in range(1, devices - 1, 2)]
        pairs = pairs + [(target, source) for source, target in pairs]
        return lax.ppermute(value, "row", pairs), swap(value, 1)

    def cross(value, other):
        return lax.ppermute(
            value, "row", [(i, (i // quads ^ other) * quads + i % quads) for i in range(devices)]
        )

    def add(one, two, kind):
        return (one.astype(f32) + two.astype(f32)).astype(kind)

    bits = []
    while 1 << len(bits) < quads:
        bits.append(1 << len(bits))

    def exchange(pieces, bit, extra=None):
        keys = sorted(key for key in pieces if key[0] & bit)
        blocks = [pieces[key] for key in keys]
        ahead, size = 0, blocks[0].shape[0]
        if extra is not None and extra.shape[1] == blocks[0].shape[1]:
            ahead = extra.shape[0]
            got = swap(jnp.concatenate([extra] + blocks, axis=0), bit)
            extra = got[:ahead]
        else:
            got = swap(jnp.concatenate(blocks, axis=0), bit)
            extra = None if extra is None else swap(extra, bit)
        kept = {key: piece for key, piece in pieces.items() if not key[0] & bit}
        for i, (target, source) in enumerate(keys):
            at = ahead + i * size
            kept[target ^ bit, source ^ bit] = got[at : at + size]
        return kept, extra

    def spread(held, bits):
        for bit in reversed(bits):
            held.update({i ^ bit: swap(block, bit) for i, block in list(held.items())})

    def near(even, odd):
        return even, swap(odd, bits[0])

    def far(even, odd):
        held = add(even, odd, f32).reshape(-1, cells, chans)
        for bit in bits[1:-1]:
            pairs = held.reshape(-1, 2, cells, chans)
            held = pairs[:, 0] + swap(pairs[:, 1].astype(bf16), bit).astype(f32)
        return held[0], held[1].astype(bf16)

    step = round_up(own, 16)
    block = layers * step
    *pieces, small, far_pack = call(
        functools.partial(pack_kernel, quads, layers, rows),
        [((block, lanes), bf16)] * (quads // 2)
        + [((rows, lanes), bf16), ((rows + quads // 2 * block, lanes), bf16)],
        (
            depth_weight.T,
            depth_bias.reshape(1, own),
            norm_gain.reshape(1, own),
            norm_shift.reshape(1, own),
            down_bias.reshape(1, own),
            up_bias.reshape(1, part),
            up_weight,
        ),
        [pltpu.VMEM((rows, own), f32), pltpu.VMEM((rows, lanes), f32)]
        + [pltpu.VMEM((own, taps), bf16)]
        + [pltpu.VMEM((1, own), bf16)] * 4
        + [pltpu.VMEM((1, part), bf16), pltpu.VMEM((own, hidden_units), bf16)]
        + [pltpu.SemaphoreType.DMA((7,))],
        space=pl.ANY,
        mib=60,
    )
    features, cotangent, down_weight = lax.optimization_barrier(
        (features, cotangent, down_weight, small)
    )[:3]
    got = swap(far_pack, bits[-1])
    pieces = {(i, 0): piece for i, piece in enumerate(pieces)}
    for i in range(quads // 2):
        pieces[i, bits[-1]] = got[rows + i * block : rows + (i + 1) * block]
    small = small + got[:rows]
    small, pieces = lax.optimization_barrier((small, pieces))
    for bit in reversed(bits[:-1]):
        pieces, got = exchange(pieces, bit, small)
        small = small + got
    small, pieces = lax.optimization_barrier((small, pieces))
    merged = share == chans and own % 16 == 0 and part % own == 0
    (up,) = call(
        functools.partial(unpack_kernel, quads, layers),
        [(((part // own if merged else 0) + quads, own, share), bf16)],
        [down_weight] + [pieces[0, i] for i in range(quads)],
    )
    up = up.reshape(-1, share)
    weights = [[up]] if merged else [[down_weight], [up]]
    for held in weights:
        held.extend(turn(held[0], step) for step in range(1, layers))
    outer, inner = halo(features)
    cots = {0: cotangent.reshape(cells, chans)}
    spread(cots, bits[1:])
    smalls = small
    other = 1
    while other < layers:
        smalls = jnp.concatenate([smalls, cross(smalls, other)], axis=0)
        other *= 2
    first = [held[1] for held in weights]
    smalls, first = lax.optimization_barrier((smalls, first))
    for held, value in zip(weights, first):
        held[1] = value
    smalls = [smalls[i * rows : (i + 1) * rows] for i in range(layers)]

    rim = (height + 6, width + 16, chans)
    normal, normed, inv, params, bias = call(
        functools.partial(conv_kernel, quads, layers),
        [
            ((cells, chans), bf16),
            ((cells, chans), f32),
            ((cells, lanes), f32),
            ((rows, chans), f32),
            ((8, share), f32),
        ],
        (features, outer, inner, *smalls),
        [pltpu.VMEM(rim, f32), pltpu.VMEM((cells, chans), f32)],
    )
    normal, cots = lax.optimization_barrier((normal, cots))
    normals = {0: normal}
    spread(normals, bits[1:])
    normals, weights = lax.optimization_barrier((normals, weights))
    spread(cots, bits[:1])
    spread(normals, bits[:1])
    normals, cots = ([held[i] for i in range(quads)] for held in (normals, cots))

    half = quads // 2 * cells
    total_up, even, odd, act, upb, down_full = call(
        functools.partial(mlp_kernel, quads, layers),
        [((chans, share), f32), ((half, chans), f32), ((half, chans), bf16)]
        + [((quads * cells, share), bf16), ((8, share), f32), ((share, chans), bf16)],
        (bias, *normals, *cots, *(block for held in weights for block in held)),
        [pltpu.VMEM((chans, share), bf16)],
        mib=40,
    )
    sums = near(even, odd)
    if merged:
        shapes = [(part + lanes, chans)] * (layers - 1)
    else:
        shapes = [(part, chans)] * (layers - 1) + [(lanes, share)] * (layers - 1)
    own_down, own_up, *sends, even, odd = call(
        functools.partial(out_kernel, quads, layers, scale),
        [((part, chans), f32), ((lanes, share), f32)]
        + [(shape, bf16) for shape in shapes]
        + [((half, chans), f32), ((half, chans), bf16)],
        (total_up, act, down_full, *cots),
        [pltpu.VMEM((share, chans), f32)],
        mib=40,
    )
    sums, sends = lax.optimization_barrier((sums, sends))
    kept, sent = far(*sums)
    dnorms = [kept, swap(sent, bits[-1])]
    terms = [turn(send, i % (layers - 1) + 1) for i, send in enumerate(sends)]
    sums = near(even, odd)
    dnorms, sums = lax.optimization_barrier((dnorms, sums))
    mixed, across = far(*sums)
    across = swap(across, bits[-1])

    dconv, norms = call(
        norm_back_kernel,
        [((height, width, chans), bf16), ((8, chans), f32)],
        (normed, inv, params, *dnorms),
    )
    (total,) = call(
        functools.partial(taps_kernel, quads, layers, scale),
        [((layers, rows, lanes), f32)],
        (dconv, features, outer, inner, cotangent, norms, upb),
        [pltpu.VMEM(rim, f32), pltpu.VMEM((rows, chans), f32)],
    )
    for bit in bits[:-1]:
        total = total + swap(total, bit)
    total, dconv, across, terms[0], terms[2:] = lax.optimization_barrier(
        (total, dconv, across, terms[0], terms[2:])
    )
    outer_back, inner_back = halo(dconv)
    total = total + swap(total, bits[-1])
    total, terms, inner_back = lax.optimization_barrier((total, terms, inner_back))
    grad_down_weight, *pieces = call(
        functools.partial(up_split_kernel, quads, part),
        [((part, chans), f32), ((own, share), f32)] + [((own, share), bf16)] * (quads - 1),
        (own_down, own_up, *terms),
    )
    pieces = {(i, 0): piece for i, piece in enumerate(pieces)}
    pieces, _ = exchange(pieces, bits[-1])
    while total.shape[0] > 2:
        middle = total.shape[0] // 2
        total = total[:middle] + cross(total[middle:], middle)
    (grad_features,) = call(
        back_kernel,
        [((height, width, chans), bf16)],
        (dconv, outer_back, inner_back, cotangent, params),
        [pltpu.VMEM(rim, f32)],
    )
    block_out = (
        features.astype(f32)
        + (mixed + across.astype(f32) + params[row_down, 0:chans]).reshape(height, width, chans)
    ).astype(bf16)
    total, grad_features, block_out, pieces = lax.optimization_barrier(
        (total, grad_features, block_out, pieces)
    )
    last = cross(total[1], 1)
    for bit in reversed(bits[:-1]):
        pieces, _ = exchange(pieces, bit)
    (grad_up_weight,) = call(
        functools.partial(up_join_kernel, quads, layers),
        [((own, hidden_units), f32)],
        [pieces[0, i] for i in range(quads)],
    )
    total, grad_up_weight = lax.optimization_barrier((total[0], grad_up_weight))
    small_outs = call(
        functools.partial(small_kernel, quads, part),
        [((own, taps), f32)] + [((1, own), f32)] * 4 + [((1, part), f32)],
        (total, last),
    )
    grad_depth_weight = small_outs[0].T
    grad_depth_bias, grad_norm_gain, grad_norm_shift, grad_down_bias, grad_up_bias = (
        value.reshape(-1) for value in small_outs[1:]
    )

    return (
        block_out,
        grad_features,
        grad_up_weight,
        grad_down_weight,
        grad_depth_weight,
        grad_depth_bias,
        grad_norm_gain,
        grad_norm_shift,
        grad_up_bias,
        grad_down_bias,
    )


def solution(mesh):
    placed = (
        P(("groups", "row"), None, None),
        P(("groups", "row"), None, None),
        P(None, "row"),
        P("row"),
        P("row"),
        P("row"),
        P("row", None),
        P("row"),
        P("row", None),
        P("row"),
    )
    return jax.shard_map(
        per_device,
        mesh=mesh,
        in_specs=placed,
        out_specs=(
            P(("groups", "row"), None, None),
            P(("groups", "row"), None, None),
            P(("groups", "row"), None),
            P(("groups", "row"), None),
            P("groups", "row"),
            P(("groups", "row")),
            P(("groups", "row")),
            P(("groups", "row")),
            P(("groups", "row")),
            P(("groups", "row")),
        ),
        check_vma=False,
    )
```

```python
import functools
import math

import jax
import jax.numpy as jnp
from jax import lax
from jax.experimental import pallas as pl
from jax.experimental.pallas import tpu as pltpu
from jax.sharding import PartitionSpec as P

eps = 1e-06
lanes = 128
taps = 49
f32 = jnp.float32
bf16 = jnp.bfloat16
row_bias, row_gain, row_shift, row_down, row_up = 49, 50, 51, 52, 53


def round_up(value, unit):
    return (value + unit - 1) // unit * unit


def call(kernel, outs, args, scratch=(), mib=24, flops=1000, moved=1000, space=pltpu.VMEM):
    return pl.pallas_call(
        kernel,
        out_shape=[jax.ShapeDtypeStruct(shape, dtype) for shape, dtype in outs],
        in_specs=[pl.BlockSpec(memory_space=space)] * len(args),
        out_specs=[pl.BlockSpec(memory_space=pltpu.VMEM)] * len(outs),
        scratch_shapes=list(scratch),
        compiler_params=pltpu.CompilerParams(vmem_limit_bytes=mib * 1024 * 1024),
        cost_estimate=pl.CostEstimate(flops=flops, bytes_accessed=moved, transcendentals=0),
    )(*args)


def place(quads):
    index = lax.axis_index("row")
    return index // quads, lax.rem(index, quads)


def one_hot(rows, columns, offset):
    down = lax.broadcasted_iota(jnp.int32, (rows, columns), 0)
    across = lax.broadcasted_iota(jnp.int32, (rows, columns), 1)
    return (across == down + offset).astype(f32)


def pack_kernel(quads, layers, rows, *refs):
    given, refs = refs[:7], refs[7:]
    near, small, far, (held, head, *local), sems = (
        refs[: quads // 2],
        refs[quads // 2],
        refs[quads // 2 + 1],
        refs[quads // 2 + 2 : -1],
        refs[-1],
    )
    copies = [
        pltpu.make_async_copy(source, target, sems.at[i])
        for i, (source, target) in enumerate(zip(given, local))
    ]
    for copy in copies:
        copy.start()
    for copy in copies:
        copy.wait()
    dw, db, gain, shift, down, upb, up = local
    _, member = place(quads)
    own = dw.shape[0]
    part = upb.shape[1]
    step = round_up(own, 16)
    spread = one_hot(own, lanes, member * own).astype(bf16)
    held[...] = jnp.zeros_like(held)
    held[row_bias : row_bias + 1, :] = db[...].astype(f32)
    held[row_gain : row_gain + 1, :] = gain[...].astype(f32)
    held[row_shift : row_shift + 1, :] = shift[...].astype(f32)
    held[row_down : row_down + 1, :] = down[...].astype(f32)
    head[...] = jnp.dot(held[...].astype(bf16), spread, preferred_element_type=f32)
    head[0:taps, :] = lax.dot_general(
        dw[...], spread, (((0,), (0,)), ((), ())), preferred_element_type=f32
    )
    for s in range(quads):
        head[row_up + s : row_up + s + 1, 0:part] = jnp.where(
            member == s, upb[...].astype(f32), 0.0
        )
    small[...] = head[...].astype(bf16)
    far[0:rows, :] = head[...].astype(bf16)
    wide = [up[:, i * part : (i + 1) * part] for i in range(layers * quads)]
    for other in range(quads):
        partner = jnp.bitwise_xor(member, other)
        if other < quads // 2:
            out, base = near[other], 0
        else:
            out, base = far, rows + (other - quads // 2) * layers * step
        if step != own or part != lanes:
            out[base : base + layers * step, :] = jnp.zeros((layers * step, lanes), bf16)
        for z in range(layers):
            piece = wide[z * quads]
            for s in range(1, quads):
                piece = jnp.where(partner == s, wide[z * quads + s], piece)
            out[base + z * step : base + z * step + own, 0:part] = piece


def unpack_kernel(quads, layers, down, *refs):
    pieces, out = refs[:-1], refs[-1]
    _, member = place(quads)
    blocks, own, share = out.shape
    ahead = blocks - quads
    part = share // layers
    step = round_up(own, 16)
    for i in range(ahead):
        out[i] = down[i * own : (i + 1) * own, :]
    for other, piece in enumerate(pieces):
        to = ahead + jnp.bitwise_xor(member, other)
        for z in range(layers):
            block = piece[z * step : (z + 1) * step, :]
            out[to, :, z * part : (z + 1) * part] = block[0:own, 0:part]


def fill(padded, block, outer, inner, width):
    height = block.shape[0]
    even = lax.rem(lax.axis_index("row"), 2) == 0
    rows, columns, chans = padded.shape
    zero = jnp.zeros((rows, 8, chans), f32)
    padded[:, 0:8, :] = zero
    padded[:, 8 + width :, :] = jnp.zeros((rows, columns - 8 - width, chans), f32)
    low = jnp.where(even, outer[height - 3 :, :, :], inner[height - 3 :, :, :])
    high = jnp.where(even, inner[0:3, :, :], outer[0:3, :, :])
    padded[0:3, 8 : 8 + width, :] = low.astype(f32)
    padded[3 : 3 + height, 8 : 8 + width, :] = block[...].astype(f32)
    padded[3 + height :, 8 : 8 + width, :] = high.astype(f32)


def slide(padded, weights, height, width, at, flip):
    tiles = (width // 8, 8, lanes)
    sums = [jnp.zeros(tiles, f32) for _ in range(height)]
    for second in range(7):
        order = [first * 7 + second for first in range(7)]
        order = [taps - 1 - tap if flip else tap for tap in order]
        held = [jnp.broadcast_to(weights[tap : tap + 1, at], tiles[1:]) for tap in order]
        for row in range(height + 6):
            piece = padded[row, 5 + second : 5 + second + width, at].reshape(tiles)
            for out in range(height):
                if 0 <= row - out < 7:
                    sums[out] = sums[out] + piece * held[row - out]
    return [value.reshape(width, lanes) for value in sums]


def conv_kernel(quads, layers, features, outer, inner, *refs):
    smalls, (normal, normed, inv, params, bias, padded, conv) = refs[:-7], refs[-7:]
    height, width, chans = features.shape
    layer, member = place(quads)
    for other, small in enumerate(smalls):
        at = pl.multiple_of(jnp.bitwise_xor(layer, other) * lanes, lanes)
        params[:, pl.ds(at, lanes)] = small[...].astype(f32)
    part = bias.shape[1] // layers
    for z in range(layers):
        at = slice(z * lanes, z * lanes + part)
        value = params[row_up : row_up + 1, at]
        for s in range(1, quads):
            value = jnp.where(member == s, params[row_up + s : row_up + s + 1, at], value)
        bias[:, z * part : (z + 1) * part] = jnp.broadcast_to(value, (8, part))
    fill(padded, features, outer, inner, width)

    def chunk(i, carry):
        at = pl.ds(pl.multiple_of(i * lanes, lanes), lanes)
        sums = slide(padded, params, height, width, at, False)
        for out in range(height):
            conv[out * width : (out + 1) * width, at] = (
                sums[out] + params[row_bias : row_bias + 1, at]
            )
        return carry

    lax.fori_loop(0, chans // lanes, chunk, 0, unroll=True)

    def norm(i, carry):
        at = pl.ds(pl.multiple_of(i * width, width), width)
        value = conv[at, :]
        centered = value - jnp.mean(value, axis=1, keepdims=True)
        var = jnp.mean(centered * centered, axis=1, keepdims=True)
        scale = lax.rsqrt(var + eps)
        value = centered * scale
        normed[at, :] = value
        inv[at, :] = jnp.broadcast_to(scale, (width, lanes))
        normal[at, :] = (
            value * params[row_gain : row_gain + 1, 0:chans]
            + params[row_shift : row_shift + 1, 0:chans]
        ).astype(bf16)
        return carry

    lax.fori_loop(0, height, norm, 0, unroll=True)


def back_kernel(dconv, outer, inner, cotangent, params, out, padded):
    height, width, chans = dconv.shape
    fill(padded, dconv, outer, inner, width)

    def chunk(i, carry):
        at = pl.ds(pl.multiple_of(i * lanes, lanes), lanes)
        sums = slide(padded, params, height, width, at, True)
        for row in range(height):
            out[row, :, at] = (cotangent[row, :, at].astype(f32) + sums[row]).astype(bf16)
        return carry

    lax.fori_loop(0, chans // lanes, chunk, 0, unroll=True)


def taps_kernel(
    quads, layers, scale, dconv, features, outer, inner, cotangent, norms, upb, *refs
):
    out, padded, grads = refs
    height, width, chans = dconv.shape
    layer, member = place(quads)
    fill(padded, features, outer, inner, width)
    grads[...] = jnp.zeros_like(grads)

    def fold(value):
        return jnp.sum(value.reshape(width // 8, 8, lanes), axis=0)

    def chunk(i, carry):
        at = pl.ds(pl.multiple_of(i * lanes, lanes), lanes)
        own = [dconv[row, :, at].astype(f32) for row in range(height)]
        for second in range(7):
            sums = [jnp.zeros((8, lanes), f32) for _ in range(7)]
            for row in range(height + 6):
                piece = padded[row, 5 + second : 5 + second + width, at]
                for out in range(height):
                    first = row - out
                    if 0 <= first < 7:
                        sums[first] = sums[first] + fold(own[out] * piece)
            for first in range(7):
                tap = first * 7 + second
                grads[tap : tap + 1, at] = (
                    jnp.sum(sums[first], axis=0, keepdims=True) * scale
                )
        total = fold(own[0])
        for row in range(1, height):
            total = total + fold(own[row])
        grads[row_bias : row_bias + 1, at] = jnp.sum(total, axis=0, keepdims=True) * scale
        total = fold(cotangent[0, :, at].astype(f32))
        for row in range(1, height):
            total = total + fold(cotangent[row, :, at].astype(f32))
        grads[row_down : row_down + 1, at] = jnp.sum(total, axis=0, keepdims=True) * scale
        grads[row_gain : row_gain + 1, at] = norms[0:1, at] * scale
        grads[row_shift : row_shift + 1, at] = norms[1:2, at] * scale
        return carry

    lax.fori_loop(0, chans // lanes, chunk, 0, unroll=True)
    part = upb.shape[1] // layers
    for z in range(layers):
        bias = upb[0:1, z * part : (z + 1) * part] * scale
        for s in range(quads):
            grads[row_up + s : row_up + s + 1, z * lanes : z * lanes + part] = jnp.where(
                member == s, bias, 0.0
            )
    for other in range(layers):
        at = pl.multiple_of(jnp.bitwise_xor(layer, other) * lanes, lanes)
        out[other] = grads[:, pl.ds(at, lanes)]


def mlp_kernel(quads, layers, bias_row, *refs):
    normals, refs = refs[:quads], refs[quads:]
    cots, refs = refs[:quads], refs[quads:]
    weights, (total, even, odd, act, upb, down, up, cells_in, slopes) = refs[:-9], refs[-9:]
    layer, _ = place(quads)
    cells, chans = normals[0].shape
    hidden_units = act.shape[1]
    part = hidden_units // layers
    for step in range(layers):
        source = lax.rem(layer - step + layers, layers)
        if len(weights) == layers:
            one, two = weights[step].at[0:part], weights[step].at[part:]
        else:
            one, two = weights[step], weights[layers + step]
        down[pl.ds(pl.multiple_of(source * part, part), part), :] = one[...]
        up[pl.ds(pl.multiple_of(source * lanes, lanes), lanes), :] = two[...]
    bias = bias_row[0:1, :]
    bias_sum = jnp.zeros((1, hidden_units), f32)
    for i in range(quads):
        hidden = jnp.dot(normals[i][...], up[...], preferred_element_type=f32) + bias
        dact = lax.dot_general(
            cots[i][...], down[...], (((1,), (1,)), ((), ())), preferred_element_type=f32
        )
        cumulative = 0.5 * (1.0 + lax.erf(hidden * (1.0 / math.sqrt(2.0))))
        density = jnp.exp(-0.5 * hidden * hidden) * (1.0 / math.sqrt(2.0 * math.pi))
        act[i * cells : (i + 1) * cells, :] = (hidden * cumulative).astype(bf16)
        dhidden = (dact * (cumulative + hidden * density)).astype(bf16)
        bias_sum = bias_sum + jnp.sum(dhidden.astype(f32), axis=0, keepdims=True)
        dnorm = lax.dot_general(
            dhidden, up[...], (((1,), (1,)), ((), ())), preferred_element_type=f32
        )
        at = slice(i // 2 * cells, (i // 2 + 1) * cells)
        if i % 2:
            odd[at, :] = dnorm.astype(bf16)
        else:
            even[at, :] = dnorm
        cells_in[i * cells : (i + 1) * cells, :] = normals[i][...]
        slopes[i * cells : (i + 1) * cells, :] = dhidden
    total[...] = lax.dot_general(
        cells_in[...], slopes[...], (((0,), (0,)), ((), ())), preferred_element_type=f32
    )
    upb[...] = jnp.broadcast_to(bias_sum, upb.shape)


def out_kernel(quads, layers, scale, total_up, act, down, *refs):
    cots, refs = refs[:quads], refs[quads:]
    own_down, own_up, refs = refs[0], refs[1], refs[2:]
    sends, (even, odd, total, held) = refs[:-4], refs[-4:]
    layer, _ = place(quads)
    cells = cots[0].shape[0]
    part = down.shape[0] // layers
    for i in range(quads):
        held[i * cells : (i + 1) * cells, :] = cots[i][...]
    total[...] = lax.dot_general(
        act[...], held[...], (((0,), (0,)), ((), ())), preferred_element_type=f32
    )
    for step in range(layers):
        if step == 0:
            one, two = own_down, own_up
        elif len(sends) == layers - 1:
            one, two = sends[step - 1].at[0:part], sends[step - 1].at[part:]
        else:
            one, two = sends[step - 1], sends[layers - 2 + step]
        to = lax.rem(layer + step, layers)
        piece = total[pl.ds(pl.multiple_of(to * part, part), part), :] * scale
        one[...] = piece.astype(one.dtype)
        piece = total_up[pl.ds(pl.multiple_of(to * lanes, lanes), lanes), :] * scale
        two[...] = piece.astype(two.dtype)
    for i in range(quads):
        block = act[i * cells : (i + 1) * cells, :]
        mixed = jnp.dot(block, down[...], preferred_element_type=f32)
        at = slice(i // 2 * cells, (i // 2 + 1) * cells)
        if i % 2:
            odd[at, :] = mixed.astype(bf16)
        else:
            even[at, :] = mixed


def norm_back_kernel(normed, inv, params, *refs):
    parts, (dconv, norms) = refs[:-2], refs[-2:]
    height, width, chans = dconv.shape
    gain_sum = jnp.zeros((1, chans), f32)
    shift_sum = jnp.zeros((1, chans), f32)
    for row in range(height):
        at = slice(row * width, (row + 1) * width)
        dnorm = parts[0][at, :].astype(f32)
        for part in parts[1:]:
            dnorm = dnorm + part[at, :].astype(f32)
        value = normed[at, :]
        gain_sum = gain_sum + jnp.sum(dnorm * value, axis=0, keepdims=True)
        shift_sum = shift_sum + jnp.sum(dnorm, axis=0, keepdims=True)
        scaled = dnorm * params[row_gain : row_gain + 1, 0:chans]
        mean = jnp.mean(scaled, axis=1, keepdims=True)
        cross = jnp.mean(scaled * value, axis=1, keepdims=True)
        dconv[row, :, :] = (inv[at, 0:1] * (scaled - mean - value * cross)).astype(bf16)
    norms[0:1, :] = gain_sum
    norms[1:2, :] = shift_sum


def up_split_kernel(quads, part, *refs):
    own_down, own_up, refs = refs[0], refs[1], refs[2:]
    terms, out_down, outs = refs[: -quads - 1], refs[-quads - 1], refs[-quads:]
    _, member = place(quads)
    if terms[0].shape[0] > lanes:
        downs = [term.at[0:part] for term in terms]
        ups = [term.at[part:] for term in terms]
    else:
        downs, ups = terms[: len(terms) // 2], terms[len(terms) // 2 :]
    total = own_down[...]
    for term in downs:
        total = total + term[...].astype(f32)
    out_down[...] = total
    own = outs[0].shape[0]
    for other, out in enumerate(outs):
        row = pl.multiple_of(jnp.bitwise_xor(member, other) * own, own)
        piece = own_up[pl.ds(row, own), :]
        for term in ups:
            piece = piece + term[pl.ds(row, own), :].astype(f32)
        out[...] = piece.astype(out.dtype)


def up_join_kernel(quads, layers, *refs):
    pieces, out = refs[:-1], refs[-1]
    _, member = place(quads)
    part = out.shape[1] // (quads * layers)
    for s in range(quads):
        held = pieces[s][...].astype(f32)
        for m in range(1, quads):
            held = jnp.where(member == m, pieces[s ^ m][...].astype(f32), held)
        for z in range(layers):
            at = (z * quads + s) * part
            out[:, at : at + part] = held[:, z * part : (z + 1) * part]


def small_kernel(quads, part_up, *refs):
    parts, outs = refs[:-6], refs[-6:]
    _, member = place(quads)
    total = parts[0][...]
    for part in parts[1:]:
        total = total + part[...]
    own = outs[0].shape[0]
    down = lax.broadcasted_iota(jnp.int32, (lanes, own), 0)
    across = lax.broadcasted_iota(jnp.int32, (lanes, own), 1)
    pick = (down == across + member * own).astype(f32)
    mine = jnp.dot(total, pick, preferred_element_type=f32, precision=lax.Precision.HIGHEST)
    outs[0][...] = lax.dot_general(
        pick,
        total[0:taps, :],
        (((0,), (1,)), ((), ())),
        preferred_element_type=f32,
        precision=lax.Precision.HIGHEST,
    )
    for row, out in zip((row_bias, row_gain, row_shift, row_down), outs[1:5]):
        out[...] = mine[row : row + 1, :]
    at = lax.broadcasted_iota(jnp.int32, total.shape, 0)
    chosen = jnp.where(at == row_up + member, total, 0.0)
    outs[5][...] = jnp.sum(chosen, axis=0, keepdims=True)[:, 0:part_up]


def per_device(
    features,
    cotangent,
    depth_weight,
    depth_bias,
    norm_gain,
    norm_shift,
    up_weight,
    up_bias,
    down_weight,
    down_bias,
):
    height, width, chans = features.shape
    devices = lax.axis_size("row")
    own, hidden_units = up_weight.shape
    part = down_weight.shape[0]
    layers = chans // lanes
    quads = devices // layers
    share = layers * part
    cells = height * width
    scale = 1.0 / math.sqrt(cells * devices)
    rows = round_up(row_up + quads, 16)

    def swap(value, other):
        return lax.ppermute(value, "row", [(i, i ^ other) for i in range(devices)])

    def turn(value, step=1):
        pairs = [
            (i, (i // quads + step) % layers * quads + i % quads) for i in range(devices)
        ]
        return lax.ppermute(value, "row", pairs)

    def halo(value):
        pairs = [(i, i + 1) for i in range(1, devices - 1, 2)]
        pairs = pairs + [(target, source) for source, target in pairs]
        return lax.ppermute(value, "row", pairs), swap(value, 1)

    def cross(value, other):
        return lax.ppermute(
            value, "row", [(i, (i // quads ^ other) * quads + i % quads) for i in range(devices)]
        )

    def add(one, two, kind):
        return (one.astype(f32) + two.astype(f32)).astype(kind)

    bits = []
    while 1 << len(bits) < quads:
        bits.append(1 << len(bits))

    def exchange(pieces, bit, extra=None):
        keys = sorted(key for key in pieces if key[0] & bit)
        blocks = [pieces[key] for key in keys]
        ahead, size = 0, blocks[0].shape[0]
        if extra is not None and extra.shape[1] == blocks[0].shape[1]:
            ahead = extra.shape[0]
            got = swap(jnp.concatenate([extra] + blocks, axis=0), bit)
            extra = got[:ahead]
        else:
            got = swap(jnp.concatenate(blocks, axis=0), bit)
            extra = None if extra is None else swap(extra, bit)
        kept = {key: piece for key, piece in pieces.items() if not key[0] & bit}
        for i, (target, source) in enumerate(keys):
            at = ahead + i * size
            kept[target ^ bit, source ^ bit] = got[at : at + size]
        return kept, extra

    def spread(held, bits):
        for bit in reversed(bits):
            held.update({i ^ bit: swap(block, bit) for i, block in list(held.items())})

    def near(even, odd):
        return even, swap(odd, bits[0])

    def far(even, odd):
        held = add(even, odd, f32).reshape(-1, cells, chans)
        for bit in bits[1:-1]:
            pairs = held.reshape(-1, 2, cells, chans)
            held = pairs[:, 0] + swap(pairs[:, 1].astype(bf16), bit).astype(f32)
        return held[0], held[1].astype(bf16)

    step = round_up(own, 16)
    block = layers * step
    *pieces, small, far_pack = call(
        functools.partial(pack_kernel, quads, layers, rows),
        [((block, lanes), bf16)] * (quads // 2)
        + [((rows, lanes), bf16), ((rows + quads // 2 * block, lanes), bf16)],
        (
            depth_weight.T,
            depth_bias.reshape(1, own),
            norm_gain.reshape(1, own),
            norm_shift.reshape(1, own),
            down_bias.reshape(1, own),
            up_bias.reshape(1, part),
            up_weight,
        ),
        [pltpu.VMEM((rows, own), f32), pltpu.VMEM((rows, lanes), f32)]
        + [pltpu.VMEM((own, taps), bf16)]
        + [pltpu.VMEM((1, own), bf16)] * 4
        + [pltpu.VMEM((1, part), bf16), pltpu.VMEM((own, hidden_units), bf16)]
        + [pltpu.SemaphoreType.DMA((7,))],
        space=pl.ANY,
        mib=60,
    )
    features, cotangent, down_weight = lax.optimization_barrier(
        (features, cotangent, down_weight, small)
    )[:3]
    got = swap(far_pack, bits[-1])
    pieces = {(i, 0): piece for i, piece in enumerate(pieces)}
    for i in range(quads // 2):
        pieces[i, bits[-1]] = got[rows + i * block : rows + (i + 1) * block]
    small = small + got[:rows]
    small, pieces = lax.optimization_barrier((small, pieces))
    for bit in reversed(bits[:-1]):
        pieces, got = exchange(pieces, bit, small)
        small = small + got
    small, pieces = lax.optimization_barrier((small, pieces))
    merged = share == chans and own % 16 == 0 and part % own == 0
    (up,) = call(
        functools.partial(unpack_kernel, quads, layers),
        [(((part // own if merged else 0) + quads, own, share), bf16)],
        [down_weight] + [pieces[0, i] for i in range(quads)],
    )
    up = up.reshape(-1, share)
    weights = [[up]] if merged else [[down_weight], [up]]
    for held in weights:
        held.extend(turn(held[0], step) for step in range(1, layers))
    outer, inner = halo(features)
    cots = {0: cotangent.reshape(cells, chans)}
    spread(cots, bits[1:])
    smalls = small
    other = 1
    while other < layers:
        smalls = jnp.concatenate([smalls, cross(smalls, other)], axis=0)
        other *= 2
    first = [held[1] for held in weights]
    smalls, first = lax.optimization_barrier((smalls, first))
    for held, value in zip(weights, first):
        held[1] = value
    smalls = [smalls[i * rows : (i + 1) * rows] for i in range(layers)]

    rim = (height + 6, width + 16, chans)
    normal, normed, inv, params, bias = call(
        functools.partial(conv_kernel, quads, layers),
        [
            ((cells, chans), bf16),
            ((cells, chans), f32),
            ((cells, lanes), f32),
            ((rows, chans), f32),
            ((8, share), f32),
        ],
        (features, outer, inner, *smalls),
        [pltpu.VMEM(rim, f32), pltpu.VMEM((cells, chans), f32)],
    )
    normal, cots = lax.optimization_barrier((normal, cots))
    normals = {0: normal}
    spread(normals, bits[1:])
    normals, weights = lax.optimization_barrier((normals, weights))
    spread(cots, bits[:1])
    spread(normals, bits[:1])
    normals, cots = ([held[i] for i in range(quads)] for held in (normals, cots))

    half = quads // 2 * cells
    total_up, even, odd, act, upb, down_full = call(
        functools.partial(mlp_kernel, quads, layers),
        [((chans, share), f32), ((half, chans), f32), ((half, chans), bf16)]
        + [((quads * cells, share), bf16), ((8, share), f32), ((share, chans), bf16)],
        (bias, *normals, *cots, *(block for held in weights for block in held)),
        [
            pltpu.VMEM((chans, share), bf16),
            pltpu.VMEM((quads * cells, chans), bf16),
            pltpu.VMEM((quads * cells, share), bf16),
        ],
        mib=40,
    )
    sums = near(even, odd)
    if merged:
        shapes = [(part + lanes, chans)] * (layers - 1)
    else:
        shapes = [(part, chans)] * (layers - 1) + [(lanes, share)] * (layers - 1)
    own_down, own_up, *sends, even, odd = call(
        functools.partial(out_kernel, quads, layers, scale),
        [((part, chans), f32), ((lanes, share), f32)]
        + [(shape, bf16) for shape in shapes]
        + [((half, chans), f32), ((half, chans), bf16)],
        (total_up, act, down_full, *cots),
        [pltpu.VMEM((share, chans), f32), pltpu.VMEM((quads * cells, chans), bf16)],
        mib=40,
    )
    sums, sends = lax.optimization_barrier((sums, sends))
    kept, sent = far(*sums)
    dnorms = [kept, swap(sent, bits[-1])]
    terms = [turn(send, i % (layers - 1) + 1) for i, send in enumerate(sends)]
    sums = near(even, odd)
    dnorms, sums = lax.optimization_barrier((dnorms, sums))
    mixed, across = far(*sums)
    across = swap(across, bits[-1])

    dconv, norms = call(
        norm_back_kernel,
        [((height, width, chans), bf16), ((8, chans), f32)],
        (normed, inv, params, *dnorms),
    )
    (total,) = call(
        functools.partial(taps_kernel, quads, layers, scale),
        [((layers, rows, lanes), f32)],
        (dconv, features, outer, inner, cotangent, norms, upb),
        [pltpu.VMEM(rim, f32), pltpu.VMEM((rows, chans), f32)],
    )
    for bit in bits[:-1]:
        total = total + swap(total, bit)
    total, dconv, across, terms[0], terms[2:] = lax.optimization_barrier(
        (total, dconv, across, terms[0], terms[2:])
    )
    outer_back, inner_back = halo(dconv)
    total = total + swap(total, bits[-1])
    total, terms, inner_back = lax.optimization_barrier((total, terms, inner_back))
    grad_down_weight, *pieces = call(
        functools.partial(up_split_kernel, quads, part),
        [((part, chans), f32), ((own, share), f32)] + [((own, share), bf16)] * (quads - 1),
        (own_down, own_up, *terms),
    )
    pieces = {(i, 0): piece for i, piece in enumerate(pieces)}
    pieces, _ = exchange(pieces, bits[-1])
    while total.shape[0] > 2:
        middle = total.shape[0] // 2
        total = total[:middle] + cross(total[middle:], middle)
    (grad_features,) = call(
        back_kernel,
        [((height, width, chans), bf16)],
        (dconv, outer_back, inner_back, cotangent, params),
        [pltpu.VMEM(rim, f32)],
    )
    block_out = (
        features.astype(f32)
        + (mixed + across.astype(f32) + params[row_down, 0:chans]).reshape(height, width, chans)
    ).astype(bf16)
    total, grad_features, block_out, pieces = lax.optimization_barrier(
        (total, grad_features, block_out, pieces)
    )
    last = cross(total[1], 1)
    for bit in reversed(bits[:-1]):
        pieces, _ = exchange(pieces, bit)
    (grad_up_weight,) = call(
        functools.partial(up_join_kernel, quads, layers),
        [((own, hidden_units), f32)],
        [pieces[0, i] for i in range(quads)],
    )
    total, grad_up_weight = lax.optimization_barrier((total[0], grad_up_weight))
    small_outs = call(
        functools.partial(small_kernel, quads, part),
        [((own, taps), f32)] + [((1, own), f32)] * 4 + [((1, part), f32)],
        (total, last),
    )
    grad_depth_weight = small_outs[0].T
    grad_depth_bias, grad_norm_gain, grad_norm_shift, grad_down_bias, grad_up_bias = (
        value.reshape(-1) for value in small_outs[1:]
    )

    return (
        block_out,
        grad_features,
        grad_up_weight,
        grad_down_weight,
        grad_depth_weight,
        grad_depth_bias,
        grad_norm_gain,
        grad_norm_shift,
        grad_up_bias,
        grad_down_bias,
    )


def solution(mesh):
    placed = (
        P(("groups", "row"), None, None),
        P(("groups", "row"), None, None),
        P(None, "row"),
        P("row"),
        P("row"),
        P("row"),
        P("row", None),
        P("row"),
        P("row", None),
        P("row"),
    )
    return jax.shard_map(
        per_device,
        mesh=mesh,
        in_specs=placed,
        out_specs=(
            P(("groups", "row"), None, None),
            P(("groups", "row"), None, None),
            P(("groups", "row"), None),
            P(("groups", "row"), None),
            P("groups", "row"),
            P(("groups", "row")),
            P(("groups", "row")),
            P(("groups", "row")),
            P(("groups", "row")),
            P(("groups", "row")),
        ),
        check_vma=False,
    )
```
